32 devices in a mesh: vox: 2 (over y), subj: 4 (over z), site: 4 (over x, core).
Axes of the slice: x: 2, y: 2, z: 4, core: 2. Of those that a mesh axis runs over, the one named last changes fastest.
Arguments:
- voxel_data: bfloat16 [2048, 8, 8, 128], P(('subj', 'site'), 'vox'), may hold values from -6 to 6
- site_label: int32 [2048], P(('subj', 'site')), may hold values from 0 to 59, as said below
- covariates: bfloat16 [2048, 40], P(('subj', 'site')), may hold values from -0.375 to 0.375
- brain_mask: int32 [8, 8, 128], P('vox'), may hold values 0 or 1
Outputs:
- cross_product: float32 [40, 8192], P(None, ('vox', 'subj', 'site'))
The draws below stay inside these ranges and needn't reach their ends.
Inputs may be any that keep to these rules, and one draw needn't show every extreme that they name: `site_label`: every site has at least 8 subjects.
All inputs are finite; a program needn't handle non-finite values. No bound on the sum of `brain_mask` on one device may be relied on, other than what follows from the above.
Results may differ from the reference program's by a relative error of at most 0.002.
The reference program's roundings to bfloat16 on the way count: a program that leaves them out, or rounds other values in their place, can miss the bound.
Values may be sent and summed in bfloat16 or wider, within the bound.
A program may use at most 64 MiB of HBM per device.

```python
import jax
import jax.numpy as jnp
from jax import lax

SUBJ_DEV = 128
NSITE = 60
COVARS = 40
VY = 8
VZ = 128
PASSES = 3
EB_ITERS = 5
SUBJECTS = 2048
NX = 8
VOXELS = 8192


def draw_site_label(key, part):
    keys = jax.random.split(jax.random.fold_in(key, 17), 5)
    spread = jax.random.randint(keys[0], (SUBJECTS,), 0, NSITE)
    busy = jax.random.randint(keys[1], (SUBJECTS,), 0, max(NSITE // 4, 1))
    pick = jax.random.randint(keys[2], (SUBJECTS,), 0, 2)
    base = jnp.where(pick == 1, busy, spread)
    order = jax.random.permutation(keys[3], SUBJECTS)
    floor_rows = order[:8 * NSITE]
    base = base.at[floor_rows].set(jnp.arange(8 * NSITE, dtype=jnp.int32) % NSITE)
    relabel = jax.random.permutation(keys[4], NSITE).astype(jnp.int32)
    return relabel[base]


def set_ends(values, rng, least, high):
    index_at = [jax.random.randint(jax.random.fold_in(rng, axis), (), 0, length) for axis, length in enumerate(values.shape)]
    main_axis = values.shape.index(max(values.shape))
    beside = index_at[:main_axis] + [(index_at[main_axis] + 1) % values.shape[main_axis]] + index_at[main_axis + 1:]
    return values.at[tuple(index_at)].set(least).at[tuple(beside)].set(high)


def block_scale(own_key, dims, cuts, smallest, top_value):
    def one(dim, blocks):
        heights = jax.random.uniform(jax.random.fold_in(jax.random.fold_in(own_key, 6), dim), (blocks,), jnp.float32, smallest / len(cuts), top_value / len(cuts))
        return jnp.repeat(jnp.exp(heights), dims[dim] // blocks).reshape((-1,) + (1,) * (len(dims) - dim - 1))

    level = one(*cuts[0])
    for cut in cuts[1:]:
        level = level * one(*cut)
    return level


def gaussian(rng, dims, scale, limit, shards=(), held_as=jnp.bfloat16):
    gain = block_scale(rng, dims, shards, -0.22, 0.18) if shards else 1.0
    values = jax.random.normal(rng, dims, jnp.float32) * scale * gain
    return jnp.minimum(jnp.maximum(values, -limit), limit).astype(held_as)


def setup_inputs(seed: int = 0) -> dict:
    streams_of = jax.random.split(jax.random.key(seed), 5)
    voxel_data = gaussian(streams_of[0], (SUBJECTS, NX, VY, VZ), 1.0, 6.0, ((0, 16), (1, 2)))
    site_label = draw_site_label(jax.random.fold_in(streams_of[4], 71), 0)
    covariates = gaussian(streams_of[2], (SUBJECTS, COVARS), (SUBJECTS // 9) ** -0.5, 0.375, ((0, 16),))
    brain_mask = set_ends((jax.random.randint(streams_of[3], (NX, VY, VZ), 0, 4) < 3).astype(jnp.int32), jax.random.fold_in(streams_of[3], 1), 0, 1)
    return {"voxel_data": voxel_data, "site_label": site_label, "covariates": covariates, "brain_mask": brain_mask}


center_weight = 0.1
along_weight = 0.35
across_weight = 0.05

def kernel_pass(extended, mask_part):
    wide = extended.astype(jnp.float32)
    core = wide[:, 1:-1]
    along = wide[:, 2:] + wide[:, :-2]
    padded = jnp.pad(core, ((0, 0), (0, 0), (1, 1), (1, 1)))
    across = padded[:, :, 2:, 1:-1] + padded[:, :, :-2, 1:-1] + padded[:, :, 1:-1, 2:] + padded[:, :, 1:-1, :-2]
    mixed = center_weight * core + along_weight * along + across_weight * across
    return (mixed * mask_part).astype(jnp.bfloat16)

def smooth(block, mask_float):
    current = block
    for step in range(PASSES):
        extended = jnp.pad(current, ((0, 0), (1, 1), (0, 0), (0, 0)))
        current = kernel_pass(extended, mask_float)
    return current

def site_stats(moments, counts):
    first = moments[0]
    second = moments[1]
    total = jnp.sum(counts)
    voxel_mean = lax.optimization_barrier(jnp.sum(first, axis=0)) / total
    voxel_var = lax.optimization_barrier(jnp.sum(second, axis=0)) / total - voxel_mean * voxel_mean + 1e-05
    column = counts[:, None]
    sum_z = (first - column * voxel_mean) / jnp.sqrt(voxel_var)
    sum_zz = (second - 2.0 * voxel_mean * first + column * voxel_mean * voxel_mean) / voxel_var
    gamma_hat = sum_z / column
    delta_hat = (sum_zz - sum_z * sum_z / column) / (column - 1.0)
    return (voxel_mean, voxel_var, sum_z, sum_zz, gamma_hat, delta_hat)

def prior_terms(gamma_hat, delta_hat, weights):
    terms = jnp.stack([lax.optimization_barrier(jnp.sum(weights * gamma_hat, axis=1)), lax.optimization_barrier(jnp.sum(weights * gamma_hat * gamma_hat, axis=1)), lax.optimization_barrier(jnp.sum(weights * delta_hat, axis=1)), lax.optimization_barrier(jnp.sum(weights * delta_hat * delta_hat, axis=1))])
    return (terms, jnp.sum(weights))

def eb_tables(terms, weight_total, counts, voxel_var, sum_z, sum_zz, gamma_hat, delta_hat):
    gamma_bar = (terms[0] / weight_total)[:, None]
    tau_sq = (terms[1] / weight_total)[:, None] - gamma_bar * gamma_bar + 1e-06
    delta_mean = (terms[2] / weight_total)[:, None]
    delta_var = (terms[3] / weight_total)[:, None] - delta_mean * delta_mean + 1e-06
    shape_a = (2.0 * delta_var + delta_mean * delta_mean) / delta_var
    shape_b = (delta_mean * delta_var + delta_mean * delta_mean * delta_mean) / delta_var
    column = counts[:, None]
    gamma_star = gamma_hat
    delta_star = delta_hat
    for step in range(EB_ITERS):
        gamma_star = (column * tau_sq * gamma_hat + delta_star * gamma_bar) / (column * tau_sq + delta_star)
        spread = sum_zz - 2.0 * gamma_star * sum_z + column * gamma_star * gamma_star
        delta_star = (shape_b + 0.5 * spread) / (0.5 * column + shape_a - 1.0)
    shift = (jnp.sqrt(voxel_var) * gamma_star).astype(jnp.bfloat16)
    scale = (1.0 / jnp.sqrt(delta_star)).astype(jnp.bfloat16)
    return (shift, scale)

def adjust(smoothed, onehot, voxel_mean, shift, scale):
    shift_at = jnp.dot(onehot, shift, preferred_element_type=jnp.float32)
    scale_at = jnp.dot(onehot, scale, preferred_element_type=jnp.float32)
    centered = smoothed.astype(jnp.float32) - voxel_mean
    return ((centered - shift_at) * scale_at + voxel_mean).astype(jnp.bfloat16)

def onehot_of(labels):
    sites = jnp.arange(NSITE, dtype=jnp.int32)
    return (labels[:, None] == sites[None, :]).astype(jnp.bfloat16)

def reference(voxel_data, site_label, covariates, brain_mask):
    blocks = SUBJECTS // SUBJ_DEV
    data_blocks = voxel_data.reshape(blocks, SUBJ_DEV, NX, VY, VZ)
    label_blocks = site_label.reshape(blocks, SUBJ_DEV)
    cov_blocks = covariates.reshape(blocks, SUBJ_DEV, COVARS)
    mask_float = brain_mask.astype(jnp.float32)

    def moment_step(carry, item):
        data, labels = item
        smoothed = smooth(data, mask_float).reshape(SUBJ_DEV, VOXELS)
        onehot = onehot_of(labels)
        wide = smoothed.astype(jnp.float32)
        square = (wide * wide).astype(jnp.bfloat16)
        first = jnp.dot(onehot.T, smoothed, preferred_element_type=jnp.float32)
        second = jnp.dot(onehot.T, square, preferred_element_type=jnp.float32)
        counts = lax.optimization_barrier(jnp.sum(onehot.astype(jnp.float32), axis=0))
        return ((carry[0] + jnp.stack([first, second]), carry[1] + counts), None)
    start = (jnp.zeros((2, NSITE, VOXELS), jnp.float32), jnp.zeros((NSITE,), jnp.float32))
    (moments, counts), unused = lax.scan(moment_step, start, (data_blocks, label_blocks))
    voxel_mean, voxel_var, sum_z, sum_zz, gamma_hat, delta_hat = site_stats(moments, counts)
    terms, weight_total = prior_terms(gamma_hat, delta_hat, mask_float.reshape(VOXELS))
    shift, scale = eb_tables(terms, weight_total, counts, voxel_var, sum_z, sum_zz, gamma_hat, delta_hat)

    def glm_step(carry, item):
        data, labels, cov = item
        smoothed = smooth(data, mask_float).reshape(SUBJ_DEV, VOXELS)
        adjusted = adjust(smoothed, onehot_of(labels), voxel_mean, shift, scale)
        return (carry + jnp.dot(cov.T, adjusted, preferred_element_type=jnp.float32), None)
    result, unused = lax.scan(glm_step, jnp.zeros((COVARS, VOXELS), jnp.float32), (data_blocks, label_blocks, cov_blocks))
    return result
```

```python
import jax
import jax.numpy as jnp
from jax import lax
from jax.sharding import PartitionSpec as P

NSITE = 60
PASSES = 3
EB_ITERS = 5


center_weight = 0.1
along_weight = 0.35
across_weight = 0.05


def kernel_pass(extended, mask_part):
    wide = extended.astype(jnp.float32)
    core = wide[:, 1:-1]
    along = wide[:, 2:] + wide[:, :-2]
    padded = jnp.pad(core, ((0, 0), (0, 0), (1, 1), (1, 1)))
    across = (
        padded[:, :, 2:, 1:-1]
        + padded[:, :, :-2, 1:-1]
        + padded[:, :, 1:-1, 2:]
        + padded[:, :, 1:-1, :-2]
    )
    mixed = center_weight * core + along_weight * along + across_weight * across
    return lax.reduce_precision(mixed * mask_part, 8, 7).astype(jnp.bfloat16)


def site_stats(moments, counts):
    first = moments[0]
    second = moments[1]
    total = jnp.sum(counts)
    voxel_mean = jnp.sum(first, axis=0) / total
    voxel_var = jnp.sum(second, axis=0) / total - voxel_mean * voxel_mean + 1e-05
    column = counts[:, None]
    sum_z = (first - column * voxel_mean) / jnp.sqrt(voxel_var)
    sum_zz = (second - 2.0 * voxel_mean * first + column * voxel_mean * voxel_mean) / voxel_var
    gamma_hat = sum_z / column
    delta_hat = (sum_zz - sum_z * sum_z / column) / (column - 1.0)
    return (voxel_mean, voxel_var, sum_z, sum_zz, gamma_hat, delta_hat)


def prior_terms(gamma_hat, delta_hat, weights):
    terms = jnp.stack(
        [
            jnp.sum(weights * gamma_hat, axis=1),
            jnp.sum(weights * gamma_hat * gamma_hat, axis=1),
            jnp.sum(weights * delta_hat, axis=1),
            jnp.sum(weights * delta_hat * delta_hat, axis=1),
        ]
    )
    return (terms, jnp.sum(weights))


def eb_tables(terms, weight_total, counts, voxel_var, sum_z, sum_zz, gamma_hat, delta_hat):
    gamma_bar = (terms[0] / weight_total)[:, None]
    tau_sq = (terms[1] / weight_total)[:, None] - gamma_bar * gamma_bar + 1e-06
    delta_mean = (terms[2] / weight_total)[:, None]
    delta_var = (terms[3] / weight_total)[:, None] - delta_mean * delta_mean + 1e-06
    shape_a = (2.0 * delta_var + delta_mean * delta_mean) / delta_var
    shape_b = (delta_mean * delta_var + delta_mean * delta_mean * delta_mean) / delta_var
    column = counts[:, None]
    gamma_star = gamma_hat
    delta_star = delta_hat
    for step in range(EB_ITERS):
        gamma_star = (column * tau_sq * gamma_hat + delta_star * gamma_bar) / (
            column * tau_sq + delta_star
        )
        spread = sum_zz - 2.0 * gamma_star * sum_z + column * gamma_star * gamma_star
        delta_star = (shape_b + 0.5 * spread) / (0.5 * column + shape_a - 1.0)
    shift = (jnp.sqrt(voxel_var) * gamma_star).astype(jnp.bfloat16)
    scale = (1.0 / jnp.sqrt(delta_star)).astype(jnp.bfloat16)
    return (shift, scale)


def widen(block, width):
    count = lax.axis_size("vox")
    forward = [(i, i + 1) for i in range(count - 1)]
    backward = [(target, source) for source, target in forward]
    low = lax.ppermute(lax.slice_in_dim(block, block.shape[1] - width, None, axis=1), "vox", forward)
    high = lax.ppermute(lax.slice_in_dim(block, 0, width, axis=1), "vox", backward)
    return jnp.concatenate([low, block, high], axis=1)


def per_device(voxel_data, site_label, covariates, brain_mask):
    group = ("subj", "site")
    rows = voxel_data.shape[0]
    tile_cells = voxel_data.shape[1] * voxel_data.shape[2] * voxel_data.shape[3]
    members = lax.axis_size(group)
    piece = tile_cells // members
    me = lax.axis_index(group)
    labels = lax.all_gather(site_label, group, tiled=True)
    covs = lax.all_gather(covariates, group, tiled=True)
    masks = widen(brain_mask.astype(jnp.bfloat16)[None], PASSES)[0].astype(jnp.float32)
    current = widen(voxel_data, PASSES)
    for step in range(PASSES):
        masks = masks[1:-1]
        current = kernel_pass(current, masks)
    smoothed = current.reshape(rows, members, piece)
    smoothed = lax.all_to_all(smoothed, group, 1, 0, tiled=True).reshape(rows * members, piece)
    sites = jnp.arange(NSITE, dtype=jnp.int32)
    onehot = (labels[:, None] == sites[None, :]).astype(jnp.bfloat16)
    wide = smoothed.astype(jnp.float32)
    square = (wide * wide).astype(jnp.bfloat16)
    first = jnp.dot(onehot.T, smoothed, preferred_element_type=jnp.float32)
    second = jnp.dot(onehot.T, square, preferred_element_type=jnp.float32)
    counts = jnp.sum(onehot.astype(jnp.float32), axis=0)
    weights = lax.dynamic_slice_in_dim(brain_mask.reshape(tile_cells), me * piece, piece, 0).astype(jnp.float32)
    stats = site_stats((first, second), counts)
    voxel_mean, voxel_var, sum_z, sum_zz, gamma_hat, delta_hat = stats
    local_terms, local_weight = prior_terms(gamma_hat, delta_hat, weights)
    packed = jnp.concatenate([local_terms, jnp.full((1, NSITE), local_weight)])
    packed = lax.psum(packed, ("vox", "subj", "site"))
    shift, scale = eb_tables(
        packed[:4], packed[4, 0], counts, voxel_var, sum_z, sum_zz, gamma_hat, delta_hat
    )
    shift_at = jnp.dot(onehot, shift, preferred_element_type=jnp.float32)
    scale_at = jnp.dot(onehot, scale, preferred_element_type=jnp.float32)
    adjusted = ((wide - voxel_mean - shift_at) * scale_at + voxel_mean).astype(jnp.bfloat16)
    return jnp.dot(covs.T, adjusted, preferred_element_type=jnp.float32)


def solution(mesh):
    in_specs = (
        P(("subj", "site"), "vox", None, None),
        P(("subj", "site")),
        P(("subj", "site"), None),
        P("vox", None, None),
    )
    out_specs = P(None, ("vox", "subj", "site"))
    return jax.shard_map(
        per_device, mesh=mesh, in_specs=in_specs, out_specs=out_specs, check_vma=False
    )
```

```python
import functools

import jax
import jax.numpy as jnp
from jax import lax
from jax.experimental import pallas as pl
from jax.experimental.pallas import tpu as pltpu
from jax.sharding import PartitionSpec as P

NSITE = 60
SITE_ROWS = 64
PASSES = 3
EB_ITERS = 5
CHUNKS = 4
SUB = 16
MESH = pl.DeviceIdType.MESH

center_weight = 0.1
along_weight = 0.35
across_weight = 0.05


def stencil(below, core, above, mask, inner_low, inner_high):
    along = above + below
    edge = jnp.zeros_like(core[:1])
    up = jnp.concatenate([core[1:], edge], axis=0)
    down = jnp.concatenate([edge, core[:-1]], axis=0)
    right = jnp.where(inner_high, pltpu.roll(core, core.shape[2] - 1, 2), 0.0)
    left = jnp.where(inner_low, pltpu.roll(core, 1, 2), 0.0)
    across = up + down + right + left
    mixed = center_weight * core + along_weight * along + across_weight * across
    return (mixed * mask).astype(jnp.bfloat16)


def body(
    covars, x, mask, mask_rows, pack, out,
    low, high, mask_low, mask_high, mask_wide, p1, p2, smooth, recv, gathered, flags, flags_t,
    tables, terms, group_terms, vox_terms,
    halo_send, halo_recv, mask_send, mask_recv, pack_send, pack_recv, data_send, data_recv,
    own_sem, term_send, term_recv, vox_send, vox_recv,
):
    layers, height, rows, width = x.shape
    chunk = rows // CHUNKS
    vox, vox_count = lax.axis_index("vox"), lax.axis_size("vox")
    nsite = lax.axis_size("site")
    members = lax.axis_size("subj") * nsite
    me = lax.axis_index("subj") * nsite + lax.axis_index("site")
    piece = layers * height // members

    def peer(step):
        return lax.rem(me + step, members)

    def group_id(index):
        return {"subj": index // nsite, "site": lax.rem(index, nsite)}

    def vox_peer(step):
        return lax.rem(vox + step, vox_count)

    barrier = pltpu.get_barrier_semaphore()

    @pl.loop(1, members)
    def _(step):
        pl.semaphore_signal(barrier, inc=1, device_id=group_id(peer(step)), device_id_type=MESH)

    @pl.loop(1, vox_count)
    def _(step):
        pl.semaphore_signal(barrier, inc=1, device_id={"vox": vox_peer(step)}, device_id_type=MESH)

    pl.semaphore_wait(barrier, members - 1 + vox_count - 1)

    def halo_up(c):
        rows_of = pl.ds(c * chunk, chunk)
        return pltpu.make_async_remote_copy(
            x.at[pl.ds(layers - PASSES, PASSES), :, rows_of], low.at[:, :, rows_of],
            halo_send.at[0, c], halo_recv.at[0, c], device_id={"vox": vox + 1}, device_id_type=MESH,
        )

    def halo_down(c):
        rows_of = pl.ds(c * chunk, chunk)
        return pltpu.make_async_remote_copy(
            x.at[pl.ds(0, PASSES), :, rows_of], high.at[:, :, rows_of],
            halo_send.at[1, c], halo_recv.at[1, c], device_id={"vox": vox - 1}, device_id_type=MESH,
        )

    mask_up = pltpu.make_async_remote_copy(
        mask.at[pl.ds(layers - PASSES, PASSES)], mask_low,
        mask_send.at[0], mask_recv.at[0], device_id={"vox": vox + 1}, device_id_type=MESH,
    )
    mask_down = pltpu.make_async_remote_copy(
        mask.at[pl.ds(0, PASSES)], mask_high,
        mask_send.at[1], mask_recv.at[1], device_id={"vox": vox - 1}, device_id_type=MESH,
    )
    has_up, has_down = vox < vox_count - 1, vox > 0

    @pl.when(has_up)
    def _():
        mask_up.start()
        for c in range(CHUNKS):
            halo_up(c).start()

    @pl.when(has_down)
    def _():
        mask_down.start()
        for c in range(CHUNKS):
            halo_down(c).start()

    def pack_copy(index):
        return pltpu.make_async_remote_copy(
            pack, gathered.at[me], pack_send, pack_recv,
            device_id=group_id(index), device_id_type=MESH,
        )

    @pl.loop(1, members)
    def _(step):
        pack_copy(peer(step)).start()

    gathered[me] = pack[...]

    @pl.when(jnp.logical_not(has_down))
    def _():
        low[...] = jnp.zeros_like(low)
        mask_low[...] = jnp.zeros_like(mask_low)

    @pl.when(jnp.logical_not(has_up))
    def _():
        high[...] = jnp.zeros_like(high)
        mask_high[...] = jnp.zeros_like(mask_high)

    @pl.when(has_down)
    def _():
        mask_up.wait_recv()

    @pl.when(has_up)
    def _():
        mask_down.wait_recv()

    def layer_of(low_ref, ref, high_ref, index):
        if index < PASSES:
            return low_ref.at[index]
        if index < PASSES + layers:
            return ref.at[index - PASSES]
        return high_ref.at[index - PASSES - layers]

    for index in range(layers + 2 * PASSES):
        values = layer_of(mask_low, mask, mask_high, index)[...]
        for y in range(height):
            mask_wide[index, y] = jnp.broadcast_to(values[y:y + 1], (SUB, width))

    lane = lax.broadcasted_iota(jnp.int32, (height, SUB, width), 2)
    inner_low, inner_high = lane > 0, lane < width - 1

    def send_piece(index, c):
        rows_of = pl.ds(c * chunk, chunk)
        return pltpu.make_async_remote_copy(
            smooth.at[pl.ds(index * piece, piece), rows_of], recv.at[me, :, rows_of],
            data_send, data_recv, device_id=group_id(index), device_id_type=MESH,
        )

    @pl.loop(0, CHUNKS)
    def _(c):
        @pl.when(has_down)
        def _():
            halo_up(c).wait_recv()

        @pl.when(has_up)
        def _():
            halo_down(c).wait_recv()

        @pl.loop(0, chunk // SUB)
        def _(b):
            rows_of = pl.ds(pl.multiple_of(c * chunk + b * SUB, SUB), SUB)
            sources = [layer_of(low, x, high, i) for i in range(layers + 2 * PASSES)]
            stage = [functools.partial(lambda ref: ref[:, rows_of], s) for s in sources]
            for step, target in enumerate((p1, p2, None)):
                count = layers + 2 * (PASSES - 1 - step)
                below = stage[0]().astype(jnp.float32)
                core = stage[1]().astype(jnp.float32)
                for i in range(count):
                    above = stage[i + 2]().astype(jnp.float32)
                    result = stencil(
                        below, core, above, mask_wide[i + 1 + step], inner_low, inner_high
                    )
                    if target is None:
                        smooth[pl.ds(i * height, height), rows_of] = result
                    else:
                        target[i] = result
                    below, core = core, above
                if target is not None:
                    stage = [functools.partial(lambda ref, k: ref[k], target, i) for i in range(count)]

        @pl.loop(1, members)
        def _(step):
            send_piece(peer(step), c).start()

    own = pltpu.make_async_copy(smooth.at[pl.ds(me * piece, piece)], recv.at[me], own_sem)
    own.start()

    others = pl.ds(0, members - 1)
    pltpu.make_async_copy(gathered.at[others], gathered.at[others], pack_recv).wait()
    site_row = lax.broadcasted_iota(jnp.int32, (width, rows), 0).astype(jnp.float32)
    counts = jnp.zeros((SITE_ROWS, 1), jnp.float32)
    for m in range(members):
        labels = gathered[m].astype(jnp.float32)[covars:covars + 1]
        flag = jnp.where(site_row == labels, 1.0, 0.0)
        counts = counts + jnp.sum(flag[:SITE_ROWS], axis=1, keepdims=True)
        flags_t[:, m * rows:(m + 1) * rows] = flag[:SITE_ROWS].astype(jnp.bfloat16)
        flags[m] = flag.T[:, :SITE_ROWS].astype(jnp.bfloat16)

    own.wait()
    pltpu.make_async_copy(recv.at[others], recv.at[others], data_recv).wait()

    firsts, seconds, weights = [], [], []
    for r in range(piece):
        data = recv[:, r].reshape(members * rows, width)
        values = data.astype(jnp.float32)
        square = (values * values).astype(jnp.bfloat16)
        firsts.append(jnp.dot(flags_t[...], data, preferred_element_type=jnp.float32))
        seconds.append(jnp.dot(flags_t[...], square, preferred_element_type=jnp.float32))
        weights.append(mask_rows[pl.ds(me * piece + r, 1), :])
    first = jnp.concatenate(firsts, axis=1)
    second = jnp.concatenate(seconds, axis=1)
    weight = jnp.concatenate(weights, axis=1)

    total = jnp.sum(counts)
    real = lax.broadcasted_iota(jnp.int32, (SITE_ROWS, 1), 0) < NSITE
    column = jnp.where(real, counts, 2.0)
    voxel_mean = jnp.sum(first, axis=0, keepdims=True) / total
    voxel_var = jnp.sum(second, axis=0, keepdims=True) / total - voxel_mean * voxel_mean + 1e-05
    deviation = jnp.sqrt(voxel_var)
    sum_z = (first - column * voxel_mean) / deviation
    sum_zz = (second - 2.0 * voxel_mean * first + column * voxel_mean * voxel_mean) / voxel_var
    gamma_hat = sum_z / column
    delta_hat = (sum_zz - sum_z * sum_z / column) / (column - 1.0)

    columns = (
        jnp.sum(weight * gamma_hat, axis=1, keepdims=True),
        jnp.sum(weight * gamma_hat * gamma_hat, axis=1, keepdims=True),
        jnp.sum(weight * delta_hat, axis=1, keepdims=True),
        jnp.sum(weight * delta_hat * delta_hat, axis=1, keepdims=True),
        jnp.broadcast_to(jnp.sum(weight, axis=1, keepdims=True), (SITE_ROWS, 1)),
    )
    place = lax.broadcasted_iota(jnp.int32, (SITE_ROWS, 128), 1)
    block = jnp.zeros((SITE_ROWS, 128), jnp.float32)
    for k, value in enumerate(columns):
        block = jnp.where(place == k, value, block)
    block = jnp.concatenate([block, jnp.zeros((128 - SITE_ROWS, 128), jnp.float32)], axis=0)
    terms[0] = block.T[:8]

    def term_copy(index):
        return pltpu.make_async_remote_copy(
            terms.at[0], group_terms.at[me], term_send, term_recv,
            device_id=group_id(index), device_id_type=MESH,
        )

    @pl.loop(1, members)
    def _(step):
        term_copy(peer(step)).start()

    group_terms[me] = terms[0]
    pltpu.make_async_copy(group_terms.at[others], group_terms.at[others], term_recv).wait()
    terms[1] = jnp.sum(group_terms[...], axis=0)

    def vox_copy(index):
        return pltpu.make_async_remote_copy(
            terms.at[1], vox_terms.at[vox], vox_send, vox_recv,
            device_id={"vox": index}, device_id_type=MESH,
        )

    @pl.loop(1, vox_count)
    def _(step):
        vox_copy(vox_peer(step)).start()

    vox_terms[vox] = terms[1]
    vox_others = pl.ds(0, vox_count - 1)
    pltpu.make_async_copy(vox_terms.at[vox_others], vox_terms.at[vox_others], vox_recv).wait()
    summed = jnp.sum(vox_terms[...], axis=0)
    summed = jnp.concatenate([summed, jnp.zeros((120, 128), jnp.float32)], axis=0).T[:SITE_ROWS]
    weight_total = summed[:, 4:5]

    gamma_bar = summed[:, 0:1] / weight_total
    tau_sq = summed[:, 1:2] / weight_total - gamma_bar * gamma_bar + 1e-06
    delta_mean = summed[:, 2:3] / weight_total
    delta_var = summed[:, 3:4] / weight_total - delta_mean * delta_mean + 1e-06
    shape_a = (2.0 * delta_var + delta_mean * delta_mean) / delta_var
    shape_b = (delta_mean * delta_var + delta_mean * delta_mean * delta_mean) / delta_var
    gamma_star, delta_star = gamma_hat, delta_hat
    for step in range(EB_ITERS):
        gamma_star = (column * tau_sq * gamma_hat + delta_star * gamma_bar) / (
            column * tau_sq + delta_star
        )
        spread = sum_zz - 2.0 * gamma_star * sum_z + column * gamma_star * gamma_star
        delta_star = (shape_b + 0.5 * spread) / (0.5 * column + shape_a - 1.0)
    cells = piece * width
    tables[:, :cells] = jnp.where(real, deviation * gamma_star, 0.0).astype(jnp.bfloat16)
    tables[:, cells:] = jnp.where(real, 1.0 / jnp.sqrt(delta_star), 0.0).astype(jnp.bfloat16)

    out[...] = jnp.zeros_like(out)

    @pl.loop(0, members)
    def _(m):
        picked = jnp.dot(flags[m], tables[...], preferred_element_type=jnp.float32)
        values = jnp.concatenate([recv[m, r] for r in range(piece)], axis=1).astype(jnp.float32)
        adjusted = (values - voxel_mean - picked[:, :cells]) * picked[:, cells:] + voxel_mean
        product = jnp.dot(
            gathered[m], adjusted.astype(jnp.bfloat16), preferred_element_type=jnp.float32
        )
        out[...] += product[:covars]

    @pl.when(has_up)
    def _():
        mask_up.wait_send()
        for c in range(CHUNKS):
            halo_up(c).wait_send()

    @pl.when(has_down)
    def _():
        mask_down.wait_send()
        for c in range(CHUNKS):
            halo_down(c).wait_send()

    pltpu.make_async_copy(gathered.at[others], gathered.at[others], pack_send).wait()
    pltpu.make_async_copy(recv.at[others], recv.at[others], data_send).wait()
    pltpu.make_async_copy(group_terms.at[others], group_terms.at[others], term_send).wait()
    pltpu.make_async_copy(vox_terms.at[vox_others], vox_terms.at[vox_others], vox_send).wait()


def per_device(voxel_data, site_label, covariates, brain_mask):
    rows, layers, height, width = voxel_data.shape
    covars = covariates.shape[1]
    members = lax.axis_size("subj") * lax.axis_size("site")
    vox_count = lax.axis_size("vox")
    piece = layers * height // members
    pack_rows = -(-(covars + 1) // 16) * 16
    x = jnp.transpose(voxel_data, (1, 2, 0, 3))
    mask = brain_mask.astype(jnp.float32)
    pack = jnp.concatenate(
        [
            covariates.T,
            site_label[None].astype(jnp.bfloat16),
            jnp.zeros((pack_rows - covars - 1, rows), jnp.bfloat16),
        ]
    )
    bf16, f32 = jnp.bfloat16, jnp.float32
    return pl.pallas_call(
        functools.partial(body, covars),
        out_shape=jax.ShapeDtypeStruct((covars, piece * width), f32),
        in_specs=[pl.BlockSpec(memory_space=pltpu.VMEM)] * 4,
        out_specs=pl.BlockSpec(memory_space=pltpu.VMEM),
        scratch_shapes=[
            pltpu.VMEM((PASSES, height, rows, width), bf16),
            pltpu.VMEM((PASSES, height, rows, width), bf16),
            pltpu.VMEM((PASSES, height, width), f32),
            pltpu.VMEM((PASSES, height, width), f32),
            pltpu.VMEM((layers + 2 * PASSES, height, SUB, width), f32),
            pltpu.VMEM((layers + 4, height, SUB, width), bf16),
            pltpu.VMEM((layers + 2, height, SUB, width), bf16),
            pltpu.VMEM((layers * height, rows, width), bf16),
            pltpu.VMEM((members, piece, rows, width), bf16),
            pltpu.VMEM((members, pack_rows, rows), bf16),
            pltpu.VMEM((members, rows, SITE_ROWS), bf16),
            pltpu.VMEM((SITE_ROWS, members * rows), bf16),
            pltpu.VMEM((SITE_ROWS, 2 * piece * width), bf16),
            pltpu.VMEM((2, 8, 128), f32),
            pltpu.VMEM((members, 8, 128), f32),
            pltpu.VMEM((vox_count, 8, 128), f32),
            pltpu.SemaphoreType.DMA((2, CHUNKS)),
            pltpu.SemaphoreType.DMA((2, CHUNKS)),
            pltpu.SemaphoreType.DMA((2,)),
            pltpu.SemaphoreType.DMA((2,)),
        ]
        + [pltpu.SemaphoreType.DMA(())] * 9,
        compiler_params=pltpu.CompilerParams(
            collective_id=0, has_side_effects=True, vmem_limit_bytes=40 * 1024 * 1024
        ),
    )(x, mask, mask.reshape(layers * height, width), pack)


def solution(mesh):
    in_specs = (
        P(("subj", "site"), "vox", None, None),
        P(("subj", "site")),
        P(("subj", "site"), None),
        P("vox", None, None),
    )
    out_specs = P(None, ("vox", "subj", "site"))
    return jax.shard_map(
        per_device, mesh=mesh, in_specs=in_specs, out_specs=out_specs, check_vma=False
    )
```

```python
import functools

import jax
import jax.numpy as jnp
from jax import lax
from jax.experimental import pallas as pl
from jax.experimental.pallas import tpu as pltpu
from jax.sharding import PartitionSpec as P

NSITE = 60
SITE_ROWS = 64
PASSES = 3
EB_ITERS = 5
CHUNKS = 8
SUB = 16
MESH = pl.DeviceIdType.MESH

center_weight = 0.1
along_weight = 0.35
across_weight = 0.05


def stencil(below, core, above, mask, inner_low, inner_high):
    along = above + below
    edge = jnp.zeros_like(core[:1])
    up = jnp.concatenate([core[1:], edge], axis=0)
    down = jnp.concatenate([edge, core[:-1]], axis=0)
    right = jnp.where(inner_high, pltpu.roll(core, core.shape[2] - 1, 2), 0.0)
    left = jnp.where(inner_low, pltpu.roll(core, 1, 2), 0.0)
    across = up + down + right + left
    mixed = center_weight * core + along_weight * along + across_weight * across
    return (mixed * mask).astype(jnp.bfloat16)


def body(
    covars, x, mask, mask_rows, pack, out,
    low, high, mask_low, mask_high, mask_wide, p1, p2, smooth, recv, gathered, covs, flags_wide,
    flags, flags_t, moments, tables, terms, all_terms,
    halo_send, halo_recv, mask_send, mask_recv, pack_send, pack_recv, data_send, data_recv,
    own_sem, term_send, term_recv,
):
    layers, height, rows, width = x.shape
    chunk = rows // CHUNKS
    vox, vox_count = lax.axis_index("vox"), lax.axis_size("vox")
    nsite = lax.axis_size("site")
    members = lax.axis_size("subj") * nsite
    me = lax.axis_index("subj") * nsite + lax.axis_index("site")
    piece = layers * height // members

    def peer(step):
        return lax.rem(me + step, members)

    def group_id(index):
        return {"subj": index // nsite, "site": lax.rem(index, nsite)}

    barrier = pltpu.get_barrier_semaphore()

    everyone = vox_count * members
    my_id = vox * members + me

    def any_id(step):
        index = lax.rem(my_id + step, everyone)
        member = lax.rem(index, members)
        return {"vox": index // members, "subj": member // nsite, "site": lax.rem(member, nsite)}

    @pl.loop(1, everyone)
    def _(step):
        pl.semaphore_signal(barrier, inc=1, device_id=any_id(step), device_id_type=MESH)

    pl.semaphore_wait(barrier, everyone - 1)

    def halo_up(c):
        rows_of = pl.ds(c * chunk, chunk)
        return pltpu.make_async_remote_copy(
            x.at[pl.ds(layers - PASSES, PASSES), :, rows_of], low.at[:, :, rows_of],
            halo_send.at[0, c], halo_recv.at[0, c], device_id={"vox": vox + 1}, device_id_type=MESH,
        )

    def halo_down(c):
        rows_of = pl.ds(c * chunk, chunk)
        return pltpu.make_async_remote_copy(
            x.at[pl.ds(0, PASSES), :, rows_of], high.at[:, :, rows_of],
            halo_send.at[1, c], halo_recv.at[1, c], device_id={"vox": vox - 1}, device_id_type=MESH,
        )

    mask_up = pltpu.make_async_remote_copy(
        mask.at[pl.ds(layers - PASSES, PASSES)], mask_low,
        mask_send.at[0], mask_recv.at[0], device_id={"vox": vox + 1}, device_id_type=MESH,
    )
    mask_down = pltpu.make_async_remote_copy(
        mask.at[pl.ds(0, PASSES)], mask_high,
        mask_send.at[1], mask_recv.at[1], device_id={"vox": vox - 1}, device_id_type=MESH,
    )
    has_up, has_down = vox < vox_count - 1, vox > 0

    @pl.when(has_up)
    def _():
        mask_up.start()
        for c in range(CHUNKS):
            halo_up(c).start()

    @pl.when(has_down)
    def _():
        mask_down.start()
        for c in range(CHUNKS):
            halo_down(c).start()

    def pack_copy(index):
        return pltpu.make_async_remote_copy(
            pack, gathered.at[me], pack_send, pack_recv,
            device_id=group_id(index), device_id_type=MESH,
        )

    @pl.loop(1, members)
    def _(step):
        pack_copy(peer(step)).start()

    gathered[me] = pack[...]

    @pl.when(jnp.logical_not(has_down))
    def _():
        low[...] = jnp.zeros_like(low)
        mask_low[...] = jnp.zeros_like(mask_low)

    @pl.when(jnp.logical_not(has_up))
    def _():
        high[...] = jnp.zeros_like(high)
        mask_high[...] = jnp.zeros_like(mask_high)

    @pl.when(has_down)
    def _():
        mask_up.wait_recv()

    @pl.when(has_up)
    def _():
        mask_down.wait_recv()

    def layer_of(low_ref, ref, high_ref, index):
        if index < PASSES:
            return low_ref.at[index]
        if index < PASSES + layers:
            return ref.at[index - PASSES]
        return high_ref.at[index - PASSES - layers]

    for index in range(layers + 2 * PASSES):
        values = layer_of(mask_low, mask, mask_high, index)[...]
        for y in range(height):
            mask_wide[index, y] = jnp.broadcast_to(values[y:y + 1], (SUB, width))

    lane = lax.broadcasted_iota(jnp.int32, (height, SUB, width), 2)
    inner_low, inner_high = lane > 0, lane < width - 1

    def send_piece(index, c):
        rows_of = pl.ds(c * chunk, chunk)
        return pltpu.make_async_remote_copy(
            smooth.at[pl.ds(index * piece, piece), rows_of], recv.at[me, :, rows_of],
            data_send, data_recv.at[c], device_id=group_id(index), device_id_type=MESH,
        )

    @pl.loop(0, CHUNKS)
    def _(c):
        @pl.when(has_down)
        def _():
            halo_up(c).wait_recv()

        @pl.when(has_up)
        def _():
            halo_down(c).wait_recv()

        @pl.loop(0, chunk // SUB)
        def _(b):
            rows_of = pl.ds(pl.multiple_of(c * chunk + b * SUB, SUB), SUB)
            sources = [layer_of(low, x, high, i) for i in range(layers + 2 * PASSES)]
            stage = [functools.partial(lambda ref: ref[:, rows_of], s) for s in sources]
            for step, target in enumerate((p1, p2, None)):
                count = layers + 2 * (PASSES - 1 - step)
                below = stage[0]().astype(jnp.float32)
                core = stage[1]().astype(jnp.float32)
                for i in range(count):
                    above = stage[i + 2]().astype(jnp.float32)
                    result = stencil(
                        below, core, above, mask_wide[i + 1 + step], inner_low, inner_high
                    )
                    if target is None:
                        smooth[pl.ds(i * height, height), rows_of] = result
                    else:
                        target[i] = result
                    below, core = core, above
                if target is not None:
                    stage = [functools.partial(lambda ref, k: ref[k], target, i) for i in range(count)]

        @pl.loop(1, members)
        def _(step):
            send_piece(peer(step), c).start()

    own = pltpu.make_async_copy(smooth.at[pl.ds(me * piece, piece)], recv.at[me], own_sem)
    own.start()

    others = pl.ds(0, members - 1)
    pltpu.make_async_copy(gathered.at[others], gathered.at[others], pack_recv).wait()
    site_row = lax.broadcasted_iota(jnp.int32, (width, rows), 0).astype(jnp.float32)
    counts = jnp.zeros((SITE_ROWS, 1), jnp.float32)
    for m in range(members):
        block = gathered[m]
        labels = block.astype(jnp.float32)[covars:covars + 1]
        flag = jnp.where(site_row == labels, 1.0, 0.0)
        counts = counts + jnp.sum(flag[:SITE_ROWS], axis=1, keepdims=True)
        turned = flag.T
        flags_wide[m] = turned
        flags[m * rows:(m + 1) * rows] = turned[:, :SITE_ROWS].astype(jnp.bfloat16)
        covs[:, m * rows:(m + 1) * rows] = block
    for c in range(CHUNKS):
        part = flags_wide[:, c * chunk:(c + 1) * chunk].reshape(members * chunk, width)
        flags_t[c] = part.T[:SITE_ROWS].astype(jnp.bfloat16)

    cells = piece * width
    moments[...] = jnp.zeros_like(moments)
    own.wait()

    @pl.loop(0, CHUNKS)
    def _(c):
        arrived = recv.at[others, :, pl.ds(0, chunk)]
        pltpu.make_async_copy(arrived, arrived, data_recv.at[c]).wait()
        rows_of = pl.ds(pl.multiple_of(c * chunk, chunk), chunk)
        data = jnp.concatenate(
            [recv[:, r, rows_of].reshape(members * chunk, width) for r in range(piece)], axis=1
        )
        values = data.astype(jnp.float32)
        square = (values * values).astype(jnp.bfloat16)
        moments[:, :cells] += jnp.dot(flags_t[c], data, preferred_element_type=jnp.float32)
        moments[:, cells:] += jnp.dot(flags_t[c], square, preferred_element_type=jnp.float32)

    first, second = moments[:, :cells], moments[:, cells:]
    weight = jnp.concatenate(
        [mask_rows[pl.ds(me * piece + r, 1), :] for r in range(piece)], axis=1
    )

    total = jnp.sum(counts)
    real = lax.broadcasted_iota(jnp.int32, (SITE_ROWS, 1), 0) < NSITE
    column = jnp.where(real, counts, 2.0)
    voxel_mean = jnp.sum(first, axis=0, keepdims=True) / total
    voxel_var = jnp.sum(second, axis=0, keepdims=True) / total - voxel_mean * voxel_mean + 1e-05
    deviation = jnp.sqrt(voxel_var)
    sum_z = (first - column * voxel_mean) / deviation
    sum_zz = (second - 2.0 * voxel_mean * first + column * voxel_mean * voxel_mean) / voxel_var
    gamma_hat = sum_z / column
    delta_hat = (sum_zz - sum_z * sum_z / column) / (column - 1.0)

    columns = (
        jnp.sum(weight * gamma_hat, axis=1, keepdims=True),
        jnp.sum(weight * gamma_hat * gamma_hat, axis=1, keepdims=True),
        jnp.sum(weight * delta_hat, axis=1, keepdims=True),
        jnp.sum(weight * delta_hat * delta_hat, axis=1, keepdims=True),
        jnp.broadcast_to(jnp.sum(weight, axis=1, keepdims=True), (SITE_ROWS, 1)),
    )
    place = lax.broadcasted_iota(jnp.int32, (SITE_ROWS, 128), 1)
    block = jnp.zeros((SITE_ROWS, 128), jnp.float32)
    for k, value in enumerate(columns):
        block = jnp.where(place == k, value, block)
    block = jnp.concatenate([block, jnp.zeros((128 - SITE_ROWS, 128), jnp.float32)], axis=0)
    terms[...] = block.T[:8]

    def term_copy(step):
        return pltpu.make_async_remote_copy(
            terms, all_terms.at[my_id], term_send, term_recv,
            device_id=any_id(step), device_id_type=MESH,
        )

    @pl.loop(1, everyone)
    def _(step):
        term_copy(step).start()

    all_terms[my_id] = terms[...]
    all_others = pl.ds(0, everyone - 1)
    pltpu.make_async_copy(all_terms.at[all_others], all_terms.at[all_others], term_recv).wait()
    summed = jnp.sum(all_terms[...], axis=0)
    summed = jnp.concatenate([summed, jnp.zeros((120, 128), jnp.float32)], axis=0).T[:SITE_ROWS]
    weight_total = summed[:, 4:5]

    gamma_bar = summed[:, 0:1] / weight_total
    tau_sq = summed[:, 1:2] / weight_total - gamma_bar * gamma_bar + 1e-06
    delta_mean = summed[:, 2:3] / weight_total
    delta_var = summed[:, 3:4] / weight_total - delta_mean * delta_mean + 1e-06
    shape_a = (2.0 * delta_var + delta_mean * delta_mean) / delta_var
    shape_b = (delta_mean * delta_var + delta_mean * delta_mean * delta_mean) / delta_var
    gamma_star, delta_star = gamma_hat, delta_hat
    prior = column * tau_sq
    pulled = prior * gamma_hat
    inverse = 1.0 / (0.5 * column + shape_a - 1.0)
    for step in range(EB_ITERS):
        gamma_star = (pulled + delta_star * gamma_bar) / (prior + delta_star)
        spread = sum_zz - 2.0 * gamma_star * sum_z + column * gamma_star * gamma_star
        delta_star = (shape_b + 0.5 * spread) * inverse
    tables[:, :cells] = jnp.where(real, deviation * gamma_star, 0.0).astype(jnp.bfloat16)
    tables[:, cells:] = jnp.where(real, 1.0 / jnp.sqrt(delta_star), 0.0).astype(jnp.bfloat16)

    pair = 2 if members % 2 == 0 else 1
    product = None
    for g in range(members // pair):
        span = slice(g * pair * rows, (g + 1) * pair * rows)
        picked = jnp.dot(flags[span], tables[...], preferred_element_type=jnp.float32)
        values = jnp.concatenate(
            [recv[g * pair:(g + 1) * pair, r].reshape(pair * rows, width) for r in range(piece)],
            axis=1,
        ).astype(jnp.float32)
        adjusted = (values - voxel_mean - picked[:, :cells]) * picked[:, cells:] + voxel_mean
        partial = jnp.dot(
            covs[:, span], adjusted.astype(jnp.bfloat16), preferred_element_type=jnp.float32
        )
        product = partial if product is None else product + partial
    out[...] = product[:covars]

    @pl.when(has_up)
    def _():
        mask_up.wait_send()
        for c in range(CHUNKS):
            halo_up(c).wait_send()

    @pl.when(has_down)
    def _():
        mask_down.wait_send()
        for c in range(CHUNKS):
            halo_down(c).wait_send()

    pltpu.make_async_copy(gathered.at[others], gathered.at[others], pack_send).wait()
    pltpu.make_async_copy(recv.at[others], recv.at[others], data_send).wait()
    pltpu.make_async_copy(all_terms.at[all_others], all_terms.at[all_others], term_send).wait()


def per_device(voxel_data, site_label, covariates, brain_mask):
    rows, layers, height, width = voxel_data.shape
    covars = covariates.shape[1]
    members = lax.axis_size("subj") * lax.axis_size("site")
    vox_count = lax.axis_size("vox")
    piece = layers * height // members
    pack_rows = -(-(covars + 1) // 16) * 16
    x = jnp.transpose(voxel_data, (1, 2, 0, 3))
    mask = brain_mask.astype(jnp.float32)
    pack = jnp.concatenate(
        [
            covariates.T,
            site_label[None].astype(jnp.bfloat16),
            jnp.zeros((pack_rows - covars - 1, rows), jnp.bfloat16),
        ]
    )
    bf16, f32 = jnp.bfloat16, jnp.float32
    return pl.pallas_call(
        functools.partial(body, covars),
        out_shape=jax.ShapeDtypeStruct((covars, piece * width), f32),
        in_specs=[pl.BlockSpec(memory_space=pltpu.VMEM)] * 4,
        out_specs=pl.BlockSpec(memory_space=pltpu.VMEM),
        scratch_shapes=[
            pltpu.VMEM((PASSES, height, rows, width), bf16),
            pltpu.VMEM((PASSES, height, rows, width), bf16),
            pltpu.VMEM((PASSES, height, width), f32),
            pltpu.VMEM((PASSES, height, width), f32),
            pltpu.VMEM((layers + 2 * PASSES, height, SUB, width), f32),
            pltpu.VMEM((layers + 4, height, SUB, width), bf16),
            pltpu.VMEM((layers + 2, height, SUB, width), bf16),
            pltpu.VMEM((layers * height, rows, width), bf16),
            pltpu.VMEM((members, piece, rows, width), bf16),
            pltpu.VMEM((members, pack_rows, rows), bf16),
            pltpu.VMEM((pack_rows, members * rows), bf16),
            pltpu.VMEM((members, rows, width), f32),
            pltpu.VMEM((members * rows, SITE_ROWS), bf16),
            pltpu.VMEM((CHUNKS, SITE_ROWS, members * rows // CHUNKS), bf16),
            pltpu.VMEM((SITE_ROWS, 2 * piece * width), f32),
            pltpu.VMEM((SITE_ROWS, 2 * piece * width), bf16),
            pltpu.VMEM((8, 128), f32),
            pltpu.VMEM((vox_count * members, 8, 128), f32),
            pltpu.SemaphoreType.DMA((2, CHUNKS)),
            pltpu.SemaphoreType.DMA((2, CHUNKS)),
            pltpu.SemaphoreType.DMA((2,)),
            pltpu.SemaphoreType.DMA((2,)),
        ]
        + [pltpu.SemaphoreType.DMA(())] * 3
        + [pltpu.SemaphoreType.DMA((CHUNKS,))]
        + [pltpu.SemaphoreType.DMA(())] * 3,
        compiler_params=pltpu.CompilerParams(
            collective_id=0, has_side_effects=True, vmem_limit_bytes=40 * 1024 * 1024
        ),
    )(x, mask, mask.reshape(layers * height, width), pack)


def solution(mesh):
    in_specs = (
        P(("subj", "site"), "vox", None, None),
        P(("subj", "site")),
        P(("subj", "site"), None),
        P("vox", None, None),
    )
    out_specs = P(None, ("vox", "subj", "site"))
    return jax.shard_map(
        per_device, mesh=mesh, in_specs=in_specs, out_specs=out_specs, check_vma=False
    )
```

```python
import functools

import jax
import jax.numpy as jnp
from jax import lax
from jax.experimental import pallas as pl
from jax.experimental.pallas import tpu as pltpu
from jax.sharding import PartitionSpec as P

NSITE = 60
SITE_ROWS = 64
PASSES = 3
EB_ITERS = 5
CHUNKS = 8
SUB = 16
MESH = pl.DeviceIdType.MESH

center_weight = 0.1
along_weight = 0.35
across_weight = 0.05


def stencil(below, core, above, mask, inner_low, inner_high):
    along = above + below
    edge = jnp.zeros_like(core[:1])
    up = jnp.concatenate([core[1:], edge], axis=0)
    down = jnp.concatenate([edge, core[:-1]], axis=0)
    right = jnp.where(inner_high, pltpu.roll(core, core.shape[2] - 1, 2), 0.0)
    left = jnp.where(inner_low, pltpu.roll(core, 1, 2), 0.0)
    across = up + down + right + left
    mixed = center_weight * core + along_weight * along + across_weight * across
    return (mixed * mask).astype(jnp.bfloat16)


def body(
    covars, x, mask, mask_rows, pack, out,
    low, high, mask_low, mask_high, mask_wide, p1, p2, smooth, recv, gathered, covs, flags_wide,
    flags, flags_t, moments, tables, terms, all_terms,
    halo_send, halo_recv, mask_send, mask_recv, pack_send, pack_recv, fan_send, fan_recv,
    data_send, data_recv,
    own_sem, term_send, term_recv,
):
    layers, height, rows, width = x.shape
    chunk = rows // CHUNKS
    vox, vox_count = lax.axis_index("vox"), lax.axis_size("vox")
    nsite = lax.axis_size("site")
    members = lax.axis_size("subj") * nsite
    me = lax.axis_index("subj") * nsite + lax.axis_index("site")
    piece = layers * height // members

    def peer(step):
        return lax.rem(me + step, members)

    def group_id(index):
        return {"subj": index // nsite, "site": lax.rem(index, nsite)}

    barrier = pltpu.get_barrier_semaphore()

    everyone = vox_count * members
    my_id = vox * members + me

    def any_id(step):
        index = lax.rem(my_id + step, everyone)
        member = lax.rem(index, members)
        return {"vox": index // members, "subj": member // nsite, "site": lax.rem(member, nsite)}

    @pl.loop(1, everyone)
    def _(step):
        pl.semaphore_signal(barrier, inc=1, device_id=any_id(step), device_id_type=MESH)

    pl.semaphore_wait(barrier, everyone - 1)

    def halo_up(c):
        rows_of = pl.ds(c * chunk, chunk)
        return pltpu.make_async_remote_copy(
            x.at[pl.ds(layers - PASSES, PASSES), :, rows_of], low.at[:, :, rows_of],
            halo_send.at[0, c], halo_recv.at[0, c], device_id={"vox": vox + 1}, device_id_type=MESH,
        )

    def halo_down(c):
        rows_of = pl.ds(c * chunk, chunk)
        return pltpu.make_async_remote_copy(
            x.at[pl.ds(0, PASSES), :, rows_of], high.at[:, :, rows_of],
            halo_send.at[1, c], halo_recv.at[1, c], device_id={"vox": vox - 1}, device_id_type=MESH,
        )

    mask_up = pltpu.make_async_remote_copy(
        mask.at[pl.ds(layers - PASSES, PASSES)], mask_low,
        mask_send.at[0], mask_recv.at[0], device_id={"vox": vox + 1}, device_id_type=MESH,
    )
    mask_down = pltpu.make_async_remote_copy(
        mask.at[pl.ds(0, PASSES)], mask_high,
        mask_send.at[1], mask_recv.at[1], device_id={"vox": vox - 1}, device_id_type=MESH,
    )
    has_up, has_down = vox < vox_count - 1, vox > 0

    @pl.when(has_up)
    def _():
        mask_up.start()
        for c in range(CHUNKS):
            halo_up(c).start()

    @pl.when(has_down)
    def _():
        mask_down.start()
        for c in range(CHUNKS):
            halo_down(c).start()

    nsubj = lax.axis_size("subj")
    subj, site = lax.axis_index("subj"), lax.axis_index("site")
    blocks = gathered.at[0, pl.ds(0, nsubj - 1)]
    lines = gathered.at[pl.ds(0, nsite - 1)]

    def pack_copy(step):
        return pltpu.make_async_remote_copy(
            pack, gathered.at[site, subj], pack_send, pack_recv,
            device_id={"subj": lax.rem(subj + step, nsubj)}, device_id_type=MESH,
        )

    def fan_copy(step):
        return pltpu.make_async_remote_copy(
            gathered.at[site], gathered.at[site], fan_send, fan_recv,
            device_id={"site": lax.rem(site + step, nsite)}, device_id_type=MESH,
        )

    @pl.loop(1, nsubj)
    def _(step):
        pack_copy(step).start()

    gathered[site, subj] = pack[...]

    @pl.when(jnp.logical_not(has_down))
    def _():
        low[...] = jnp.zeros_like(low)
        mask_low[...] = jnp.zeros_like(mask_low)

    @pl.when(jnp.logical_not(has_up))
    def _():
        high[...] = jnp.zeros_like(high)
        mask_high[...] = jnp.zeros_like(mask_high)

    @pl.when(has_down)
    def _():
        mask_up.wait_recv()

    @pl.when(has_up)
    def _():
        mask_down.wait_recv()

    def layer_of(low_ref, ref, high_ref, index):
        if index < PASSES:
            return low_ref.at[index]
        if index < PASSES + layers:
            return ref.at[index - PASSES]
        return high_ref.at[index - PASSES - layers]

    for index in range(layers + 2 * PASSES):
        values = layer_of(mask_low, mask, mask_high, index)[...]
        for y in range(height):
            mask_wide[index, y] = jnp.broadcast_to(values[y:y + 1], (SUB, width))

    lane = lax.broadcasted_iota(jnp.int32, (height, SUB, width), 2)
    inner_low, inner_high = lane > 0, lane < width - 1

    def send_piece(index, c):
        rows_of = pl.ds(c * chunk, chunk)
        return pltpu.make_async_remote_copy(
            smooth.at[pl.ds(index * piece, piece), rows_of], recv.at[me, :, rows_of],
            data_send, data_recv.at[c], device_id=group_id(index), device_id_type=MESH,
        )

    @pl.loop(0, CHUNKS)
    def _(c):
        @pl.when(has_down)
        def _():
            halo_up(c).wait_recv()

        @pl.when(has_up)
        def _():
            halo_down(c).wait_recv()

        @pl.loop(0, chunk // SUB)
        def _(b):
            rows_of = pl.ds(pl.multiple_of(c * chunk + b * SUB, SUB), SUB)
            sources = [layer_of(low, x, high, i) for i in range(layers + 2 * PASSES)]
            stage = [functools.partial(lambda ref: ref[:, rows_of], s) for s in sources]
            for step, target in enumerate((p1, p2, None)):
                count = layers + 2 * (PASSES - 1 - step)
                below = stage[0]().astype(jnp.float32)
                core = stage[1]().astype(jnp.float32)
                for i in range(count):
                    above = stage[i + 2]().astype(jnp.float32)
                    result = stencil(
                        below, core, above, mask_wide[i + 1 + step], inner_low, inner_high
                    )
                    if target is None:
                        smooth[pl.ds(i * height, height), rows_of] = result
                    else:
                        target[i] = result
                    below, core = core, above
                if target is not None:
                    stage = [functools.partial(lambda ref, k: ref[k], target, i) for i in range(count)]

        @pl.loop(1, members)
        def _(step):
            send_piece(peer(members - step), c).start()

        @pl.when(c == 0)
        def _():
            pltpu.make_async_copy(blocks, blocks, pack_recv).wait()

            @pl.loop(1, nsite)
            def _(step):
                fan_copy(step).start()

    own = pltpu.make_async_copy(smooth.at[pl.ds(me * piece, piece)], recv.at[me], own_sem)
    own.start()

    others = pl.ds(0, members - 1)
    pltpu.make_async_copy(lines, lines, fan_recv).wait()
    site_row = lax.broadcasted_iota(jnp.int32, (width, rows), 0).astype(jnp.float32)
    counts = jnp.zeros((SITE_ROWS, 1), jnp.float32)
    for m in range(members):
        block = gathered[m % nsite, m // nsite]
        labels = block.astype(jnp.float32)[covars:covars + 1]
        flag = jnp.where(site_row == labels, 1.0, 0.0)
        counts = counts + jnp.sum(flag[:SITE_ROWS], axis=1, keepdims=True)
        turned = flag.T
        flags_wide[m] = turned
        flags[m * rows:(m + 1) * rows] = turned[:, :SITE_ROWS].astype(jnp.bfloat16)
        covs[:, m * rows:(m + 1) * rows] = block
    for c in range(CHUNKS):
        part = flags_wide[:, c * chunk:(c + 1) * chunk].reshape(members * chunk, width)
        flags_t[c] = part.T[:SITE_ROWS].astype(jnp.bfloat16)

    cells = piece * width
    moments[...] = jnp.zeros_like(moments)
    own.wait()

    @pl.loop(0, CHUNKS)
    def _(c):
        arrived = recv.at[others, :, pl.ds(0, chunk)]
        pltpu.make_async_copy(arrived, arrived, data_recv.at[c]).wait()
        rows_of = pl.ds(pl.multiple_of(c * chunk, chunk), chunk)
        data = jnp.concatenate(
            [recv[:, r, rows_of].reshape(members * chunk, width) for r in range(piece)], axis=1
        )
        values = data.astype(jnp.float32)
        square = (values * values).astype(jnp.bfloat16)
        moments[:, :cells] += jnp.dot(flags_t[c], data, preferred_element_type=jnp.float32)
        moments[:, cells:] += jnp.dot(flags_t[c], square, preferred_element_type=jnp.float32)

    first, second = moments[:, :cells], moments[:, cells:]
    weight = jnp.concatenate(
        [mask_rows[pl.ds(me * piece + r, 1), :] for r in range(piece)], axis=1
    )

    total = jnp.sum(counts)
    real = lax.broadcasted_iota(jnp.int32, (SITE_ROWS, 1), 0) < NSITE
    column = jnp.where(real, counts, 2.0)
    voxel_mean = jnp.sum(first, axis=0, keepdims=True) / total
    voxel_var = jnp.sum(second, axis=0, keepdims=True) / total - voxel_mean * voxel_mean + 1e-05
    deviation = jnp.sqrt(voxel_var)
    sum_z = (first - column * voxel_mean) / deviation
    sum_zz = (second - 2.0 * voxel_mean * first + column * voxel_mean * voxel_mean) / voxel_var
    gamma_hat = sum_z / column
    delta_hat = (sum_zz - sum_z * sum_z / column) / (column - 1.0)

    gammas = weight * gamma_hat
    deltas = weight * delta_hat
    gamma_sums = jnp.concatenate(
        [
            jnp.sum(gammas, axis=1, keepdims=True),
            jnp.sum(gammas * gamma_hat, axis=1, keepdims=True),
        ]
    )
    delta_sums = jnp.concatenate(
        [
            jnp.sum(deltas, axis=1, keepdims=True),
            jnp.sum(deltas * delta_hat, axis=1, keepdims=True),
        ]
    )
    row = lax.broadcasted_iota(jnp.int32, (2 * SITE_ROWS, 1), 0)
    gamma_sums = jnp.where(row == NSITE, jnp.sum(weight, axis=1, keepdims=True), gamma_sums)
    place = lax.broadcasted_iota(jnp.int32, (128, 128), 1)
    block = jnp.where(place == 0, gamma_sums, jnp.where(place == 1, delta_sums, 0.0))
    terms[...] = block.T[:2]

    def term_copy(step):
        return pltpu.make_async_remote_copy(
            terms, all_terms.at[my_id], term_send, term_recv,
            device_id=any_id(step), device_id_type=MESH,
        )

    @pl.loop(1, everyone)
    def _(step):
        term_copy(step).start()

    all_terms[my_id] = terms[...]
    all_others = pl.ds(0, everyone - 1)
    pltpu.make_async_copy(all_terms.at[all_others], all_terms.at[all_others], term_recv).wait()
    summed = jnp.sum(all_terms[...], axis=0)
    weight_total = summed[0:1, NSITE:NSITE + 1]
    summed = jnp.concatenate([summed, jnp.zeros((126, 128), jnp.float32)], axis=0).T

    gamma_bar = summed[:SITE_ROWS, 0:1] / weight_total
    tau_sq = summed[SITE_ROWS:, 0:1] / weight_total - gamma_bar * gamma_bar + 1e-06
    delta_mean = summed[:SITE_ROWS, 1:2] / weight_total
    delta_var = summed[SITE_ROWS:, 1:2] / weight_total - delta_mean * delta_mean + 1e-06
    shape_a = (2.0 * delta_var + delta_mean * delta_mean) / delta_var
    shape_b = (delta_mean * delta_var + delta_mean * delta_mean * delta_mean) / delta_var
    gamma_star, delta_star = gamma_hat, delta_hat
    prior = column * tau_sq
    pulled = prior * gamma_hat
    inverse = 1.0 / (0.5 * column + shape_a - 1.0)
    for step in range(EB_ITERS):
        gamma_star = (pulled + delta_star * gamma_bar) / (prior + delta_star)
        spread = sum_zz - 2.0 * gamma_star * sum_z + column * gamma_star * gamma_star
        delta_star = (shape_b + 0.5 * spread) * inverse
    tables[:, :cells] = jnp.where(real, deviation * gamma_star, 0.0).astype(jnp.bfloat16)
    tables[:, cells:] = jnp.where(real, 1.0 / jnp.sqrt(delta_star), 0.0).astype(jnp.bfloat16)

    pair = 2 if members % 2 == 0 else 1
    product = None
    for g in range(members // pair):
        span = slice(g * pair * rows, (g + 1) * pair * rows)
        picked = jnp.dot(flags[span], tables[...], preferred_element_type=jnp.float32)
        values = jnp.concatenate(
            [recv[g * pair:(g + 1) * pair, r].reshape(pair * rows, width) for r in range(piece)],
            axis=1,
        ).astype(jnp.float32)
        adjusted = (values - voxel_mean - picked[:, :cells]) * picked[:, cells:] + voxel_mean
        partial = jnp.dot(
            covs[:, span], adjusted.astype(jnp.bfloat16), preferred_element_type=jnp.float32
        )
        product = partial if product is None else product + partial
    out[...] = product[:covars]

    @pl.when(has_up)
    def _():
        mask_up.wait_send()
        for c in range(CHUNKS):
            halo_up(c).wait_send()

    @pl.when(has_down)
    def _():
        mask_down.wait_send()
        for c in range(CHUNKS):
            halo_down(c).wait_send()

    pltpu.make_async_copy(blocks, blocks, pack_send).wait()
    pltpu.make_async_copy(lines, lines, fan_send).wait()
    pltpu.make_async_copy(recv.at[others], recv.at[others], data_send).wait()
    pltpu.make_async_copy(all_terms.at[all_others], all_terms.at[all_others], term_send).wait()


def per_device(voxel_data, site_label, covariates, brain_mask):
    rows, layers, height, width = voxel_data.shape
    covars = covariates.shape[1]
    members = lax.axis_size("subj") * lax.axis_size("site")
    vox_count = lax.axis_size("vox")
    piece = layers * height // members
    pack_rows = -(-(covars + 1) // 16) * 16
    x = jnp.transpose(voxel_data, (1, 2, 0, 3))
    mask = brain_mask.astype(jnp.float32)
    pack = jnp.concatenate(
        [
            covariates.T,
            site_label[None].astype(jnp.bfloat16),
            jnp.zeros((pack_rows - covars - 1, rows), jnp.bfloat16),
        ]
    )
    bf16, f32 = jnp.bfloat16, jnp.float32
    return pl.pallas_call(
        functools.partial(body, covars),
        out_shape=jax.ShapeDtypeStruct((covars, piece * width), f32),
        in_specs=[pl.BlockSpec(memory_space=pltpu.VMEM)] * 4,
        out_specs=pl.BlockSpec(memory_space=pltpu.VMEM),
        scratch_shapes=[
            pltpu.VMEM((PASSES, height, rows, width), bf16),
            pltpu.VMEM((PASSES, height, rows, width), bf16),
            pltpu.VMEM((PASSES, height, width), f32),
            pltpu.VMEM((PASSES, height, width), f32),
            pltpu.VMEM((layers + 2 * PASSES, height, SUB, width), f32),
            pltpu.VMEM((layers + 4, height, SUB, width), bf16),
            pltpu.VMEM((layers + 2, height, SUB, width), bf16),
            pltpu.VMEM((layers * height, rows, width), bf16),
            pltpu.VMEM((members, piece, rows, width), bf16),
            pltpu.VMEM((lax.axis_size("site"), lax.axis_size("subj"), pack_rows, rows), bf16),
            pltpu.VMEM((pack_rows, members * rows), bf16),
            pltpu.VMEM((members, rows, width), f32),
            pltpu.VMEM((members * rows, SITE_ROWS), bf16),
            pltpu.VMEM((CHUNKS, SITE_ROWS, members * rows // CHUNKS), bf16),
            pltpu.VMEM((SITE_ROWS, 2 * piece * width), f32),
            pltpu.VMEM((SITE_ROWS, 2 * piece * width), bf16),
            pltpu.VMEM((2, 128), f32),
            pltpu.VMEM((vox_count * members, 2, 128), f32),
            pltpu.SemaphoreType.DMA((2, CHUNKS)),
            pltpu.SemaphoreType.DMA((2, CHUNKS)),
            pltpu.SemaphoreType.DMA((2,)),
            pltpu.SemaphoreType.DMA((2,)),
        ]
        + [pltpu.SemaphoreType.DMA(())] * 5
        + [pltpu.SemaphoreType.DMA((CHUNKS,))]
        + [pltpu.SemaphoreType.DMA(())] * 3,
        compiler_params=pltpu.CompilerParams(
            collective_id=0, has_side_effects=True, vmem_limit_bytes=40 * 1024 * 1024
        ),
    )(x, mask, mask.reshape(layers * height, width), pack)


def solution(mesh):
    in_specs = (
        P(("subj", "site"), "vox", None, None),
        P(("subj", "site")),
        P(("subj", "site"), None),
        P("vox", None, None),
    )
    out_specs = P(None, ("vox", "subj", "site"))
    return jax.shard_map(
        per_device, mesh=mesh, in_specs=in_specs, out_specs=out_specs, check_vma=False
    )
```

```python
import functools

import jax
import jax.numpy as jnp
from jax import lax
from jax.experimental import pallas as pl
from jax.experimental.pallas import tpu as pltpu
from jax.sharding import PartitionSpec as P

NSITE = 60
SITE_ROWS = 64
PASSES = 3
EB_ITERS = 5
CHUNKS = 8
SUB = 16
MESH = pl.DeviceIdType.MESH

center_weight = 0.1
along_weight = 0.35
across_weight = 0.05


def stencil(below, core, above, mask, inner_low, inner_high):
    along = above + below
    edge = jnp.zeros_like(core[:1])
    up = jnp.concatenate([core[1:], edge], axis=0)
    down = jnp.concatenate([edge, core[:-1]], axis=0)
    right = jnp.where(inner_high, pltpu.roll(core, core.shape[2] - 1, 2), 0.0)
    left = jnp.where(inner_low, pltpu.roll(core, 1, 2), 0.0)
    across = up + down + right + left
    mixed = center_weight * core + along_weight * along + across_weight * across
    return (mixed * mask).astype(jnp.bfloat16)


def body(
    covars, x, mask, mask_rows, pack, out,
    low, high, mask_low, mask_high, mask_wide, p1, p2, smooth, recv, gathered, covs, flags_wide,
    flags, flags_t, moments, tables, centered, terms, all_terms,
    halo_send, halo_recv, mask_send, mask_recv, pack_send, pack_recv, fan_send, fan_recv,
    data_send, data_recv,
    own_sem, term_send, term_recv,
):
    layers, height, rows, width = x.shape
    chunk = rows // CHUNKS
    vox, vox_count = lax.axis_index("vox"), lax.axis_size("vox")
    nsite = lax.axis_size("site")
    members = lax.axis_size("subj") * nsite
    me = lax.axis_index("subj") * nsite + lax.axis_index("site")
    piece = layers * height // members

    def peer(step):
        return lax.rem(me + step, members)

    def group_id(index):
        return {"subj": index // nsite, "site": lax.rem(index, nsite)}

    barrier = pltpu.get_barrier_semaphore()

    everyone = vox_count * members
    my_id = vox * members + me

    def any_id(step):
        index = lax.rem(my_id + step, everyone)
        member = lax.rem(index, members)
        return {"vox": index // members, "subj": member // nsite, "site": lax.rem(member, nsite)}

    @pl.loop(1, everyone)
    def _(step):
        pl.semaphore_signal(barrier, inc=1, device_id=any_id(step), device_id_type=MESH)

    pl.semaphore_wait(barrier, everyone - 1)

    def halo_up(c):
        rows_of = pl.ds(c * chunk, chunk)
        return pltpu.make_async_remote_copy(
            x.at[pl.ds(layers - PASSES, PASSES), :, rows_of], low.at[:, :, rows_of],
            halo_send.at[0, c], halo_recv.at[0, c], device_id={"vox": vox + 1}, device_id_type=MESH,
        )

    def halo_down(c):
        rows_of = pl.ds(c * chunk, chunk)
        return pltpu.make_async_remote_copy(
            x.at[pl.ds(0, PASSES), :, rows_of], high.at[:, :, rows_of],
            halo_send.at[1, c], halo_recv.at[1, c], device_id={"vox": vox - 1}, device_id_type=MESH,
        )

    mask_up = pltpu.make_async_remote_copy(
        mask.at[pl.ds(layers - PASSES, PASSES)], mask_low,
        mask_send.at[0], mask_recv.at[0], device_id={"vox": vox + 1}, device_id_type=MESH,
    )
    mask_down = pltpu.make_async_remote_copy(
        mask.at[pl.ds(0, PASSES)], mask_high,
        mask_send.at[1], mask_recv.at[1], device_id={"vox": vox - 1}, device_id_type=MESH,
    )
    has_up, has_down = vox < vox_count - 1, vox > 0

    @pl.when(has_up)
    def _():
        mask_up.start()
        for c in range(CHUNKS):
            halo_up(c).start()

    @pl.when(has_down)
    def _():
        mask_down.start()
        for c in range(CHUNKS):
            halo_down(c).start()

    nsubj = lax.axis_size("subj")
    subj, site = lax.axis_index("subj"), lax.axis_index("site")
    blocks = gathered.at[0, pl.ds(0, nsubj - 1)]
    lines = gathered.at[pl.ds(0, nsite - 1)]

    def pack_copy(step):
        return pltpu.make_async_remote_copy(
            pack, gathered.at[site, subj], pack_send, pack_recv,
            device_id={"subj": lax.rem(subj + step, nsubj)}, device_id_type=MESH,
        )

    def fan_copy(step):
        return pltpu.make_async_remote_copy(
            gathered.at[site], gathered.at[site], fan_send, fan_recv,
            device_id={"site": lax.rem(site + step, nsite)}, device_id_type=MESH,
        )

    @pl.loop(1, nsubj)
    def _(step):
        pack_copy(step).start()

    gathered[site, subj] = pack[...]

    @pl.when(jnp.logical_not(has_down))
    def _():
        low[...] = jnp.zeros_like(low)
        mask_low[...] = jnp.zeros_like(mask_low)

    @pl.when(jnp.logical_not(has_up))
    def _():
        high[...] = jnp.zeros_like(high)
        mask_high[...] = jnp.zeros_like(mask_high)

    @pl.when(has_down)
    def _():
        mask_up.wait_recv()

    @pl.when(has_up)
    def _():
        mask_down.wait_recv()

    def layer_of(low_ref, ref, high_ref, index):
        if index < PASSES:
            return low_ref.at[index]
        if index < PASSES + layers:
            return ref.at[index - PASSES]
        return high_ref.at[index - PASSES - layers]

    for index in range(layers + 2 * PASSES):
        values = layer_of(mask_low, mask, mask_high, index)[...]
        for y in range(height):
            mask_wide[index, y] = jnp.broadcast_to(values[y:y + 1], (SUB, width))

    lane = lax.broadcasted_iota(jnp.int32, (height, SUB, width), 2)
    inner_low, inner_high = lane > 0, lane < width - 1

    def send_piece(index, c):
        rows_of = pl.ds(c * chunk, chunk)
        return pltpu.make_async_remote_copy(
            smooth.at[pl.ds(index * piece, piece), rows_of], recv.at[me, :, rows_of],
            data_send, data_recv.at[c], device_id=group_id(index), device_id_type=MESH,
        )

    @pl.loop(0, CHUNKS)
    def _(c):
        @pl.when(has_down)
        def _():
            halo_up(c).wait_recv()

        @pl.when(has_up)
        def _():
            halo_down(c).wait_recv()

        @pl.loop(0, chunk // SUB)
        def _(b):
            rows_of = pl.ds(pl.multiple_of(c * chunk + b * SUB, SUB), SUB)
            sources = [layer_of(low, x, high, i) for i in range(layers + 2 * PASSES)]
            stage = [functools.partial(lambda ref: ref[:, rows_of], s) for s in sources]
            for step, target in enumerate((p1, p2, None)):
                count = layers + 2 * (PASSES - 1 - step)
                below = stage[0]().astype(jnp.float32)
                core = stage[1]().astype(jnp.float32)
                for i in range(count):
                    above = stage[i + 2]().astype(jnp.float32)
                    result = stencil(
                        below, core, above, mask_wide[i + 1 + step], inner_low, inner_high
                    )
                    if target is None:
                        smooth[pl.ds(i * height, height), rows_of] = result
                    else:
                        target[i] = result
                    below, core = core, above
                if target is not None:
                    stage = [functools.partial(lambda ref, k: ref[k], target, i) for i in range(count)]

        @pl.loop(1, members)
        def _(step):
            send_piece(peer(members - step), c).start()

        @pl.when(c == 0)
        def _():
            pltpu.make_async_copy(blocks, blocks, pack_recv).wait()

            @pl.loop(1, nsite)
            def _(step):
                fan_copy(step).start()

    own = pltpu.make_async_copy(smooth.at[pl.ds(me * piece, piece)], recv.at[me], own_sem)
    own.start()

    others = pl.ds(0, members - 1)
    pltpu.make_async_copy(lines, lines, fan_recv).wait()
    site_row = lax.broadcasted_iota(jnp.int32, (width, rows), 0).astype(jnp.float32)
    counts = jnp.zeros((SITE_ROWS, 1), jnp.float32)
    for m in range(members):
        block = gathered[m % nsite, m // nsite]
        labels = block.astype(jnp.float32)[covars:covars + 1]
        flag = jnp.where(site_row == labels, 1.0, 0.0)
        counts = counts + jnp.sum(flag[:SITE_ROWS], axis=1, keepdims=True)
        turned = flag.T
        flags_wide[m] = turned
        flags[m * rows:(m + 1) * rows] = turned[:, :SITE_ROWS].astype(jnp.bfloat16)
        covs[:, m * rows:(m + 1) * rows] = block
    for c in range(CHUNKS):
        part = flags_wide[:, c * chunk:(c + 1) * chunk].reshape(members * chunk, width)
        flags_t[c] = part.T[:SITE_ROWS].astype(jnp.bfloat16)

    cells = piece * width
    moments[...] = jnp.zeros_like(moments)
    own.wait()

    @pl.loop(0, CHUNKS)
    def _(c):
        arrived = recv.at[others, :, pl.ds(0, chunk)]
        pltpu.make_async_copy(arrived, arrived, data_recv.at[c]).wait()
        rows_of = pl.ds(pl.multiple_of(c * chunk, chunk), chunk)
        data = jnp.concatenate(
            [recv[:, r, rows_of].reshape(members * chunk, width) for r in range(piece)], axis=1
        )
        values = data.astype(jnp.float32)
        square = (values * values).astype(jnp.bfloat16)
        moments[:, :cells] += jnp.dot(flags_t[c], data, preferred_element_type=jnp.float32)
        moments[:, cells:] += jnp.dot(flags_t[c], square, preferred_element_type=jnp.float32)

    first, second = moments[:, :cells], moments[:, cells:]
    weight = jnp.concatenate(
        [mask_rows[pl.ds(me * piece + r, 1), :] for r in range(piece)], axis=1
    )

    total = jnp.sum(counts)
    real = lax.broadcasted_iota(jnp.int32, (SITE_ROWS, 1), 0) < NSITE
    column = jnp.where(real, counts, 2.0)
    voxel_mean = jnp.sum(first, axis=0, keepdims=True) / total
    voxel_var = jnp.sum(second, axis=0, keepdims=True) / total - voxel_mean * voxel_mean + 1e-05
    deviation = jnp.sqrt(voxel_var)
    sum_z = (first - column * voxel_mean) / deviation
    sum_zz = (second - 2.0 * voxel_mean * first + column * voxel_mean * voxel_mean) / voxel_var
    gamma_hat = sum_z / column
    delta_hat = (sum_zz - sum_z * sum_z / column) / (column - 1.0)

    gammas = weight * gamma_hat
    deltas = weight * delta_hat
    gamma_sums = jnp.concatenate(
        [
            jnp.sum(gammas, axis=1, keepdims=True),
            jnp.sum(gammas * gamma_hat, axis=1, keepdims=True),
        ]
    )
    delta_sums = jnp.concatenate(
        [
            jnp.sum(deltas, axis=1, keepdims=True),
            jnp.sum(deltas * delta_hat, axis=1, keepdims=True),
        ]
    )
    row = lax.broadcasted_iota(jnp.int32, (2 * SITE_ROWS, 1), 0)
    gamma_sums = jnp.where(row == NSITE, jnp.sum(weight, axis=1, keepdims=True), gamma_sums)
    place = lax.broadcasted_iota(jnp.int32, (128, 128), 1)
    block = jnp.where(place == 0, gamma_sums, jnp.where(place == 1, delta_sums, 0.0))
    terms[...] = block.T[:2]

    def term_copy(step):
        return pltpu.make_async_remote_copy(
            terms, all_terms.at[my_id], term_send, term_recv,
            device_id=any_id(step), device_id_type=MESH,
        )

    @pl.loop(1, everyone)
    def _(step):
        term_copy(everyone - step).start()

    all_terms[my_id] = terms[...]

    pair = 2 if members % 2 == 0 else 1
    for g in range(members // pair):
        values = jnp.concatenate(
            [recv[g * pair:(g + 1) * pair, r].reshape(pair * rows, width) for r in range(piece)],
            axis=1,
        ).astype(jnp.float32)
        centered[g * pair * rows:(g + 1) * pair * rows] = values - voxel_mean

    all_others = pl.ds(0, everyone - 1)
    pltpu.make_async_copy(all_terms.at[all_others], all_terms.at[all_others], term_recv).wait()
    summed = jnp.sum(all_terms[...], axis=0)
    weight_total = summed[0:1, NSITE:NSITE + 1]
    summed = jnp.concatenate([summed, jnp.zeros((126, 128), jnp.float32)], axis=0).T

    gamma_bar = summed[:SITE_ROWS, 0:1] / weight_total
    tau_sq = summed[SITE_ROWS:, 0:1] / weight_total - gamma_bar * gamma_bar + 1e-06
    delta_mean = summed[:SITE_ROWS, 1:2] / weight_total
    delta_var = summed[SITE_ROWS:, 1:2] / weight_total - delta_mean * delta_mean + 1e-06
    shape_a = (2.0 * delta_var + delta_mean * delta_mean) / delta_var
    shape_b = (delta_mean * delta_var + delta_mean * delta_mean * delta_mean) / delta_var
    gamma_star, delta_star = gamma_hat, delta_hat
    prior = column * tau_sq
    pulled = prior * gamma_hat
    inverse = 1.0 / (0.5 * column + shape_a - 1.0)
    for step in range(EB_ITERS):
        gamma_star = (pulled + delta_star * gamma_bar) / (prior + delta_star)
        spread = sum_zz - 2.0 * gamma_star * sum_z + column * gamma_star * gamma_star
        delta_star = (shape_b + 0.5 * spread) * inverse
    tables[:, :cells] = jnp.where(real, deviation * gamma_star, 0.0).astype(jnp.bfloat16)
    tables[:, cells:] = jnp.where(real, 1.0 / jnp.sqrt(delta_star), 0.0).astype(jnp.bfloat16)

    product = None
    for g in range(members // pair):
        span = slice(g * pair * rows, (g + 1) * pair * rows)
        picked = jnp.dot(flags[span], tables[...], preferred_element_type=jnp.float32)
        adjusted = (centered[span] - picked[:, :cells]) * picked[:, cells:] + voxel_mean
        partial = jnp.dot(
            covs[:, span], adjusted.astype(jnp.bfloat16), preferred_element_type=jnp.float32
        )
        product = partial if product is None else product + partial
    out[...] = product[:covars]

    @pl.when(has_up)
    def _():
        mask_up.wait_send()
        for c in range(CHUNKS):
            halo_up(c).wait_send()

    @pl.when(has_down)
    def _():
        mask_down.wait_send()
        for c in range(CHUNKS):
            halo_down(c).wait_send()

    pltpu.make_async_copy(blocks, blocks, pack_send).wait()
    pltpu.make_async_copy(lines, lines, fan_send).wait()
    pltpu.make_async_copy(recv.at[others], recv.at[others], data_send).wait()
    pltpu.make_async_copy(all_terms.at[all_others], all_terms.at[all_others], term_send).wait()


def per_device(voxel_data, site_label, covariates, brain_mask):
    rows, layers, height, width = voxel_data.shape
    covars = covariates.shape[1]
    members = lax.axis_size("subj") * lax.axis_size("site")
    vox_count = lax.axis_size("vox")
    piece = layers * height // members
    pack_rows = -(-(covars + 1) // 16) * 16
    x = jnp.transpose(voxel_data, (1, 2, 0, 3))
    mask = brain_mask.astype(jnp.float32)
    pack = jnp.concatenate(
        [
            covariates.T,
            site_label[None].astype(jnp.bfloat16),
            jnp.zeros((pack_rows - covars - 1, rows), jnp.bfloat16),
        ]
    )
    bf16, f32 = jnp.bfloat16, jnp.float32
    return pl.pallas_call(
        functools.partial(body, covars),
        out_shape=jax.ShapeDtypeStruct((covars, piece * width), f32),
        in_specs=[pl.BlockSpec(memory_space=pltpu.VMEM)] * 4,
        out_specs=pl.BlockSpec(memory_space=pltpu.VMEM),
        scratch_shapes=[
            pltpu.VMEM((PASSES, height, rows, width), bf16),
            pltpu.VMEM((PASSES, height, rows, width), bf16),
            pltpu.VMEM((PASSES, height, width), f32),
            pltpu.VMEM((PASSES, height, width), f32),
            pltpu.VMEM((layers + 2 * PASSES, height, SUB, width), f32),
            pltpu.VMEM((layers + 4, height, SUB, width), bf16),
            pltpu.VMEM((layers + 2, height, SUB, width), bf16),
            pltpu.VMEM((layers * height, rows, width), bf16),
            pltpu.VMEM((members, piece, rows, width), bf16),
            pltpu.VMEM((lax.axis_size("site"), lax.axis_size("subj"), pack_rows, rows), bf16),
            pltpu.VMEM((pack_rows, members * rows), bf16),
            pltpu.VMEM((members, rows, width), f32),
            pltpu.VMEM((members * rows, SITE_ROWS), bf16),
            pltpu.VMEM((CHUNKS, SITE_ROWS, members * rows // CHUNKS), bf16),
            pltpu.VMEM((SITE_ROWS, 2 * piece * width), f32),
            pltpu.VMEM((SITE_ROWS, 2 * piece * width), bf16),
            pltpu.VMEM((members * rows, piece * width), f32),
            pltpu.VMEM((2, 128), f32),
            pltpu.VMEM((vox_count * members, 2, 128), f32),
            pltpu.SemaphoreType.DMA((2, CHUNKS)),
            pltpu.SemaphoreType.DMA((2, CHUNKS)),
            pltpu.SemaphoreType.DMA((2,)),
            pltpu.SemaphoreType.DMA((2,)),
        ]
        + [pltpu.SemaphoreType.DMA(())] * 5
        + [pltpu.SemaphoreType.DMA((CHUNKS,))]
        + [pltpu.SemaphoreType.DMA(())] * 3,
        compiler_params=pltpu.CompilerParams(
            collective_id=0, has_side_effects=True, vmem_limit_bytes=40 * 1024 * 1024
        ),
    )(x, mask, mask.reshape(layers * height, width), pack)


def solution(mesh):
    in_specs = (
        P(("subj", "site"), "vox", None, None),
        P(("subj", "site")),
        P(("subj", "site"), None),
        P("vox", None, None),
    )
    out_specs = P(None, ("vox", "subj", "site"))
    return jax.shard_map(
        per_device, mesh=mesh, in_specs=in_specs, out_specs=out_specs, check_vma=False
    )
```

```python
import functools

import jax
import jax.numpy as jnp
from jax import lax
from jax.experimental import pallas as pl
from jax.experimental.pallas import tpu as pltpu
from jax.sharding import PartitionSpec as P

NSITE = 60
SITE_ROWS = 64
PASSES = 3
EB_ITERS = 5
CHUNKS = 8
SUB = 16
MESH = pl.DeviceIdType.MESH

center_weight = 0.1
along_weight = 0.35
across_weight = 0.05


def stencil(below, core, above, mask, inner_low, inner_high):
    along = above + below
    edge = jnp.zeros_like(core[:1])
    up = jnp.concatenate([core[1:], edge], axis=0)
    down = jnp.concatenate([edge, core[:-1]], axis=0)
    right = jnp.where(inner_high, pltpu.roll(core, core.shape[2] - 1, 2), 0.0)
    left = jnp.where(inner_low, pltpu.roll(core, 1, 2), 0.0)
    across = up + down + right + left
    mixed = center_weight * core + along_weight * along + across_weight * across
    return (mixed * mask).astype(jnp.bfloat16)


def body(
    covars, x, mask, mask_rows, pack, out,
    low, high, mask_low, mask_high, mask_wide, p1, p2, smooth, recv, gathered, covs, flags_wide,
    flags, flags_t, moments, tables, terms, all_terms,
    halo_send, halo_recv, mask_send, mask_recv, pack_send, pack_recv, fan_send, fan_recv,
    data_send, data_recv,
    own_sem, term_send, term_recv,
):
    layers, height, rows, width = x.shape
    chunk = rows // CHUNKS
    vox, vox_count = lax.axis_index("vox"), lax.axis_size("vox")
    nsite = lax.axis_size("site")
    members = lax.axis_size("subj") * nsite
    me = lax.axis_index("subj") * nsite + lax.axis_index("site")
    piece = layers * height // members

    def peer(step):
        return lax.rem(me + step, members)

    def group_id(index):
        return {"subj": index // nsite, "site": lax.rem(index, nsite)}

    barrier = pltpu.get_barrier_semaphore()

    everyone = vox_count * members
    my_id = vox * members + me

    def any_id(step):
        index = lax.rem(my_id + step, everyone)
        member = lax.rem(index, members)
        return {"vox": index // members, "subj": member // nsite, "site": lax.rem(member, nsite)}

    @pl.loop(1, everyone)
    def _(step):
        pl.semaphore_signal(barrier, inc=1, device_id=any_id(step), device_id_type=MESH)

    pl.semaphore_wait(barrier, everyone - 1)

    def halo_up(c):
        rows_of = pl.ds(c * chunk, chunk)
        return pltpu.make_async_remote_copy(
            x.at[pl.ds(layers - PASSES, PASSES), :, rows_of], low.at[:, :, rows_of],
            halo_send.at[0, c], halo_recv.at[0, c], device_id={"vox": vox + 1}, device_id_type=MESH,
        )

    def halo_down(c):
        rows_of = pl.ds(c * chunk, chunk)
        return pltpu.make_async_remote_copy(
            x.at[pl.ds(0, PASSES), :, rows_of], high.at[:, :, rows_of],
            halo_send.at[1, c], halo_recv.at[1, c], device_id={"vox": vox - 1}, device_id_type=MESH,
        )

    mask_up = pltpu.make_async_remote_copy(
        mask.at[pl.ds(layers - PASSES, PASSES)], mask_low,
        mask_send.at[0], mask_recv.at[0], device_id={"vox": vox + 1}, device_id_type=MESH,
    )
    mask_down = pltpu.make_async_remote_copy(
        mask.at[pl.ds(0, PASSES)], mask_high,
        mask_send.at[1], mask_recv.at[1], device_id={"vox": vox - 1}, device_id_type=MESH,
    )
    has_up, has_down = vox < vox_count - 1, vox > 0

    @pl.when(has_up)
    def _():
        mask_up.start()
        for c in range(CHUNKS):
            halo_up(c).start()

    @pl.when(has_down)
    def _():
        mask_down.start()
        for c in range(CHUNKS):
            halo_down(c).start()

    nsubj = lax.axis_size("subj")
    subj, site = lax.axis_index("subj"), lax.axis_index("site")
    blocks = gathered.at[0, pl.ds(0, nsubj - 1)]
    lines = gathered.at[pl.ds(0, nsite - 1)]

    def pack_copy(step):
        return pltpu.make_async_remote_copy(
            pack, gathered.at[site, subj], pack_send, pack_recv,
            device_id={"subj": lax.rem(subj + step, nsubj)}, device_id_type=MESH,
        )

    def fan_copy(step):
        return pltpu.make_async_remote_copy(
            gathered.at[site], gathered.at[site], fan_send, fan_recv,
            device_id={"site": lax.rem(site + step, nsite)}, device_id_type=MESH,
        )

    @pl.loop(1, nsubj)
    def _(step):
        pack_copy(step).start()

    gathered[site, subj] = pack[...]

    @pl.when(jnp.logical_not(has_down))
    def _():
        low[...] = jnp.zeros_like(low)
        mask_low[...] = jnp.zeros_like(mask_low)

    @pl.when(jnp.logical_not(has_up))
    def _():
        high[...] = jnp.zeros_like(high)
        mask_high[...] = jnp.zeros_like(mask_high)

    @pl.when(has_down)
    def _():
        mask_up.wait_recv()

    @pl.when(has_up)
    def _():
        mask_down.wait_recv()

    def layer_of(low_ref, ref, high_ref, index):
        if index < PASSES:
            return low_ref.at[index]
        if index < PASSES + layers:
            return ref.at[index - PASSES]
        return high_ref.at[index - PASSES - layers]

    for index in range(layers + 2 * PASSES):
        values = layer_of(mask_low, mask, mask_high, index)[...]
        for y in range(height):
            mask_wide[index, y] = jnp.broadcast_to(values[y:y + 1], (SUB, width))

    lane = lax.broadcasted_iota(jnp.int32, (height, SUB, width), 2)
    inner_low, inner_high = lane > 0, lane < width - 1

    def send_piece(index, c):
        rows_of = pl.ds(c * chunk, chunk)
        return pltpu.make_async_remote_copy(
            smooth.at[pl.ds(index * piece, piece), rows_of], recv.at[me, :, rows_of],
            data_send, data_recv.at[c], device_id=group_id(index), device_id_type=MESH,
        )

    @pl.loop(0, CHUNKS)
    def _(c):
        @pl.when(has_down)
        def _():
            halo_up(c).wait_recv()

        @pl.when(has_up)
        def _():
            halo_down(c).wait_recv()

        @pl.loop(0, chunk // SUB)
        def _(b):
            rows_of = pl.ds(pl.multiple_of(c * chunk + b * SUB, SUB), SUB)
            sources = [layer_of(low, x, high, i) for i in range(layers + 2 * PASSES)]
            stage = [functools.partial(lambda ref: ref[:, rows_of], s) for s in sources]
            for step, target in enumerate((p1, p2, None)):
                count = layers + 2 * (PASSES - 1 - step)
                below = stage[0]().astype(jnp.float32)
                core = stage[1]().astype(jnp.float32)
                for i in range(count):
                    above = stage[i + 2]().astype(jnp.float32)
                    result = stencil(
                        below, core, above, mask_wide[i + 1 + step], inner_low, inner_high
                    )
                    if target is None:
                        smooth[pl.ds(i * height, height), rows_of] = result
                    else:
                        target[i] = result
                    below, core = core, above
                if target is not None:
                    stage = [functools.partial(lambda ref, k: ref[k], target, i) for i in range(count)]

        for away in sorted(range(nsubj), key=lambda d: -min(d, nsubj - d)):
            line = lax.rem(subj + away, nsubj) * nsite

            @pl.loop(0 if away else 1, nsite)
            def _(step):
                send_piece(line + lax.rem(site + step, nsite), c).start()

        @pl.when(c == 0)
        def _():
            pltpu.make_async_copy(blocks, blocks, pack_recv).wait()

            @pl.loop(1, nsite)
            def _(step):
                fan_copy(step).start()

    own = pltpu.make_async_copy(smooth.at[pl.ds(me * piece, piece)], recv.at[me], own_sem)
    own.start()

    others = pl.ds(0, members - 1)
    pltpu.make_async_copy(lines, lines, fan_recv).wait()
    site_row = lax.broadcasted_iota(jnp.int32, (width, rows), 0).astype(jnp.float32)
    counts = jnp.zeros((SITE_ROWS, 1), jnp.float32)
    for m in range(members):
        block = gathered[m % nsite, m // nsite]
        labels = block.astype(jnp.float32)[covars:covars + 1]
        flag = jnp.where(site_row == labels, 1.0, 0.0)
        counts = counts + jnp.sum(flag[:SITE_ROWS], axis=1, keepdims=True)
        turned = flag.T
        flags_wide[m] = turned
        flags[m * rows:(m + 1) * rows] = turned[:, :SITE_ROWS].astype(jnp.bfloat16)
        covs[:, m * rows:(m + 1) * rows] = block
    for c in range(CHUNKS):
        part = flags_wide[:, c * chunk:(c + 1) * chunk].reshape(members * chunk, width)
        flags_t[c] = part.T[:SITE_ROWS].astype(jnp.bfloat16)

    cells = piece * width
    moments[...] = jnp.zeros_like(moments)
    own.wait()

    @pl.loop(0, CHUNKS)
    def _(c):
        arrived = recv.at[others, :, pl.ds(0, chunk)]
        pltpu.make_async_copy(arrived, arrived, data_recv.at[c]).wait()
        rows_of = pl.ds(pl.multiple_of(c * chunk, chunk), chunk)
        data = jnp.concatenate(
            [recv[:, r, rows_of].reshape(members * chunk, width) for r in range(piece)], axis=1
        )
        values = data.astype(jnp.float32)
        square = (values * values).astype(jnp.bfloat16)
        moments[:, :cells] += jnp.dot(flags_t[c], data, preferred_element_type=jnp.float32)
        moments[:, cells:] += jnp.dot(flags_t[c], square, preferred_element_type=jnp.float32)

    first, second = moments[:, :cells], moments[:, cells:]
    weight = jnp.concatenate(
        [mask_rows[pl.ds(me * piece + r, 1), :] for r in range(piece)], axis=1
    )

    total = jnp.sum(counts)
    real = lax.broadcasted_iota(jnp.int32, (SITE_ROWS, 1), 0) < NSITE
    column = jnp.where(real, counts, 2.0)
    voxel_mean = jnp.sum(first, axis=0, keepdims=True) / total
    voxel_var = jnp.sum(second, axis=0, keepdims=True) / total - voxel_mean * voxel_mean + 1e-05
    deviation = jnp.sqrt(voxel_var)
    sum_z = (first - column * voxel_mean) / deviation
    sum_zz = (second - 2.0 * voxel_mean * first + column * voxel_mean * voxel_mean) / voxel_var
    gamma_hat = sum_z / column
    delta_hat = (sum_zz - sum_z * sum_z / column) / (column - 1.0)

    gammas = weight * gamma_hat
    deltas = weight * delta_hat
    gamma_sums = jnp.concatenate(
        [
            jnp.sum(gammas, axis=1, keepdims=True),
            jnp.sum(gammas * gamma_hat, axis=1, keepdims=True),
        ]
    )
    delta_sums = jnp.concatenate(
        [
            jnp.sum(deltas, axis=1, keepdims=True),
            jnp.sum(deltas * delta_hat, axis=1, keepdims=True),
        ]
    )
    row = lax.broadcasted_iota(jnp.int32, (2 * SITE_ROWS, 1), 0)
    gamma_sums = jnp.where(row == NSITE, jnp.sum(weight, axis=1, keepdims=True), gamma_sums)
    place = lax.broadcasted_iota(jnp.int32, (128, 128), 1)
    block = jnp.where(place == 0, gamma_sums, jnp.where(place == 1, delta_sums, 0.0))
    terms[...] = block.T[:2]

    def term_copy(step):
        return pltpu.make_async_remote_copy(
            terms, all_terms.at[my_id], term_send, term_recv,
            device_id=any_id(step), device_id_type=MESH,
        )

    @pl.loop(1, everyone)
    def _(step):
        term_copy(step).start()

    all_terms[my_id] = terms[...]
    all_others = pl.ds(0, everyone - 1)
    pltpu.make_async_copy(all_terms.at[all_others], all_terms.at[all_others], term_recv).wait()
    summed = jnp.sum(all_terms[...], axis=0)
    weight_total = summed[0:1, NSITE:NSITE + 1]
    summed = jnp.concatenate([summed, jnp.zeros((126, 128), jnp.float32)], axis=0).T

    gamma_bar = summed[:SITE_ROWS, 0:1] / weight_total
    tau_sq = summed[SITE_ROWS:, 0:1] / weight_total - gamma_bar * gamma_bar + 1e-06
    delta_mean = summed[:SITE_ROWS, 1:2] / weight_total
    delta_var = summed[SITE_ROWS:, 1:2] / weight_total - delta_mean * delta_mean + 1e-06
    shape_a = (2.0 * delta_var + delta_mean * delta_mean) / delta_var
    shape_b = (delta_mean * delta_var + delta_mean * delta_mean * delta_mean) / delta_var
    gamma_star, delta_star = gamma_hat, delta_hat
    prior = column * tau_sq
    pulled = prior * gamma_hat
    inverse = 1.0 / (0.5 * column + shape_a - 1.0)
    for step in range(EB_ITERS):
        gamma_star = (pulled + delta_star * gamma_bar) / (prior + delta_star)
        spread = sum_zz - 2.0 * gamma_star * sum_z + column * gamma_star * gamma_star
        delta_star = (shape_b + 0.5 * spread) * inverse
    tables[:, :cells] = jnp.where(real, deviation * gamma_star, 0.0).astype(jnp.bfloat16)
    tables[:, cells:] = jnp.where(real, 1.0 / jnp.sqrt(delta_star), 0.0).astype(jnp.bfloat16)

    pair = 2 if members % 2 == 0 else 1
    product = None
    for g in range(members // pair):
        span = slice(g * pair * rows, (g + 1) * pair * rows)
        picked = jnp.dot(flags[span], tables[...], preferred_element_type=jnp.float32)
        values = jnp.concatenate(
            [recv[g * pair:(g + 1) * pair, r].reshape(pair * rows, width) for r in range(piece)],
            axis=1,
        ).astype(jnp.float32)
        adjusted = (values - voxel_mean - picked[:, :cells]) * picked[:, cells:] + voxel_mean
        partial = jnp.dot(
            covs[:, span], adjusted.astype(jnp.bfloat16), preferred_element_type=jnp.float32
        )
        product = partial if product is None else product + partial
    out[...] = product[:covars]

    @pl.when(has_up)
    def _():
        mask_up.wait_send()
        for c in range(CHUNKS):
            halo_up(c).wait_send()

    @pl.when(has_down)
    def _():
        mask_down.wait_send()
        for c in range(CHUNKS):
            halo_down(c).wait_send()

    pltpu.make_async_copy(blocks, blocks, pack_send).wait()
    pltpu.make_async_copy(lines, lines, fan_send).wait()
    pltpu.make_async_copy(recv.at[others], recv.at[others], data_send).wait()
    pltpu.make_async_copy(all_terms.at[all_others], all_terms.at[all_others], term_send).wait()


def per_device(voxel_data, site_label, covariates, brain_mask):
    rows, layers, height, width = voxel_data.shape
    covars = covariates.shape[1]
    members = lax.axis_size("subj") * lax.axis_size("site")
    vox_count = lax.axis_size("vox")
    piece = layers * height // members
    pack_rows = -(-(covars + 1) // 16) * 16
    x = jnp.transpose(voxel_data, (1, 2, 0, 3))
    mask = brain_mask.astype(jnp.float32)
    pack = jnp.concatenate(
        [
            covariates.T,
            site_label[None].astype(jnp.bfloat16),
            jnp.zeros((pack_rows - covars - 1, rows), jnp.bfloat16),
        ]
    )
    bf16, f32 = jnp.bfloat16, jnp.float32
    return pl.pallas_call(
        functools.partial(body, covars),
        out_shape=jax.ShapeDtypeStruct((covars, piece * width), f32),
        in_specs=[pl.BlockSpec(memory_space=pltpu.VMEM)] * 4,
        out_specs=pl.BlockSpec(memory_space=pltpu.VMEM),
        scratch_shapes=[
            pltpu.VMEM((PASSES, height, rows, width), bf16),
            pltpu.VMEM((PASSES, height, rows, width), bf16),
            pltpu.VMEM((PASSES, height, width), f32),
            pltpu.VMEM((PASSES, height, width), f32),
            pltpu.VMEM((layers + 2 * PASSES, height, SUB, width), f32),
            pltpu.VMEM((layers + 4, height, SUB, width), bf16),
            pltpu.VMEM((layers + 2, height, SUB, width), bf16),
            pltpu.VMEM((layers * height, rows, width), bf16),
            pltpu.VMEM((members, piece, rows, width), bf16),
            pltpu.VMEM((lax.axis_size("site"), lax.axis_size("subj"), pack_rows, rows), bf16),
            pltpu.VMEM((pack_rows, members * rows), bf16),
            pltpu.VMEM((members, rows, width), f32),
            pltpu.VMEM((members * rows, SITE_ROWS), bf16),
            pltpu.VMEM((CHUNKS, SITE_ROWS, members * rows // CHUNKS), bf16),
            pltpu.VMEM((SITE_ROWS, 2 * piece * width), f32),
            pltpu.VMEM((SITE_ROWS, 2 * piece * width), bf16),
            pltpu.VMEM((2, 128), f32),
            pltpu.VMEM((vox_count * members, 2, 128), f32),
            pltpu.SemaphoreType.DMA((2, CHUNKS)),
            pltpu.SemaphoreType.DMA((2, CHUNKS)),
            pltpu.SemaphoreType.DMA((2,)),
            pltpu.SemaphoreType.DMA((2,)),
        ]
        + [pltpu.SemaphoreType.DMA(())] * 5
        + [pltpu.SemaphoreType.DMA((CHUNKS,))]
        + [pltpu.SemaphoreType.DMA(())] * 3,
        compiler_params=pltpu.CompilerParams(
            collective_id=0, has_side_effects=True, vmem_limit_bytes=40 * 1024 * 1024
        ),
    )(x, mask, mask.reshape(layers * height, width), pack)


def solution(mesh):
    in_specs = (
        P(("subj", "site"), "vox", None, None),
        P(("subj", "site")),
        P(("subj", "site"), None),
        P("vox", None, None),
    )
    out_specs = P(None, ("vox", "subj", "site"))
    return jax.shard_map(
        per_device, mesh=mesh, in_specs=in_specs, out_specs=out_specs, check_vma=False
    )
```
